32 devices in a mesh: uly: 8 (over z, y), blk: 4 (over x, core).
Axes of the slice: x: 2, y: 2, z: 4, core: 2. Of those that a mesh axis runs over, the one named last changes fastest.
Arguments:
- qkv: bfloat16 [8192, 6144], P(('blk', 'uly')), may hold values from -16 to 16
- tile_list: int32 [32, 8], P('blk'), may hold values from 0 to 31, as said below
Outputs:
- attended: bfloat16 [8192, 2048], P(('blk', 'uly'))
The draws below stay inside these ranges and needn't reach their ends.
Inputs may be any that keep to these rules, and one draw needn't show every extreme that they name: Let the frame of tile t be t // 8, its row t % 8 // 4 and its column t % 4. Each row of tile_list names 8 distinct tiles: its own tile and others whose frame, row and column each differ from its own by at most one.
All inputs are finite; a program needn't handle non-finite values.
Results may differ from the reference program's by a relative error of at most 0.0047.
Values may be sent and summed in bfloat16 or wider, within the bound.
A program may use at most 128 MiB of HBM per device.

```python
import math
import jax
import jax.numpy as jnp
from jax import lax

HEADS = 32
HEAD_DIM = 64
TILE = 256
LISTED = 8
TCOLS = 4
TOKENS = 8192
TILES = 32
FRAME_TILES = 8


def draw_qkv(key, part):
    shape = (TOKENS, HEADS, 3, HEAD_DIM)
    values = jnp.clip(jax.random.normal(key, shape, jnp.float32), -6.0, 6.0)
    return values.reshape(TOKENS, HEADS * 3 * HEAD_DIM).astype(jnp.bfloat16)


def draw_tile_list(key, part):
    tiles = jnp.arange(TILES, dtype=jnp.int32)
    frame = tiles // FRAME_TILES
    row_of = tiles % FRAME_TILES // TCOLS
    column = tiles % TCOLS
    offsets = jnp.arange(27, dtype=jnp.int32)
    frame_step = offsets // 9 - 1
    row_step = offsets // 3 % 3 - 1
    column_step = offsets % 3 - 1
    new_frame = frame[:, None] + frame_step[None, :]
    new_row = row_of[:, None] + row_step[None, :]
    new_column = column[:, None] + column_step[None, :]
    frames = TILES // FRAME_TILES
    rows_per = FRAME_TILES // TCOLS
    valid = (new_frame >= 0) & (new_frame < frames) & (new_row >= 0) & (new_row < rows_per) & (new_column >= 0) & (new_column < TCOLS)
    neighbour = new_frame * FRAME_TILES + new_row * TCOLS + new_column
    ranking = jax.random.randint(key, (TILES, 27), 0, 2 ** 20) * 32 + offsets[None, :]
    ranking = jnp.where(valid, ranking, -1)
    ranking = jnp.where((offsets == 13)[None, :], 2 ** 30, ranking)
    _, picked = lax.top_k(ranking, LISTED)
    return jnp.take_along_axis(neighbour, picked, axis=1).astype(jnp.int32)


def setup_inputs(seed: int = 0) -> dict:
    keys = jax.random.split(jax.random.key(seed), 3)
    return {
        "qkv": draw_qkv(jax.random.fold_in(keys[2], 71), 0),
        "tile_list": draw_tile_list(jax.random.fold_in(keys[2], 71), 0),
    }


def reference(qkv, tile_list):
    score_scale = HEAD_DIM ** -0.5
    by_head = qkv.reshape(TOKENS, HEADS, 3 * HEAD_DIM)
    group_size = math.gcd(TILES, 16)
    list_groups = tile_list.reshape(TILES // group_size, group_size, LISTED)

    def one_head(head_index):
        block = lax.dynamic_index_in_dim(by_head, head_index, 1, keepdims=False).astype(jnp.float32)
        queries = block[:, :HEAD_DIM].reshape(TILES // group_size, group_size, TILE, HEAD_DIM)
        keyvals = block[:, HEAD_DIM:].reshape(TILES, TILE, 2 * HEAD_DIM)

        def run_group(inputs):
            query_part, listed = inputs
            picked = keyvals[listed]
            scores = jnp.einsum("gqd,gjkd->gqjk", query_part, picked[..., :HEAD_DIM]) * score_scale
            row_max = jnp.max(scores, axis=(2, 3), keepdims=True)
            exponent = jnp.exp(scores - row_max)
            row_sum = jnp.sum(exponent, axis=(2, 3))
            weights = lax.optimization_barrier(exponent.astype(jnp.bfloat16)).astype(jnp.float32)
            summed = jnp.einsum("gqjk,gjkd->gqd", weights, picked[..., HEAD_DIM:])
            return (summed / row_sum[..., None]).astype(jnp.bfloat16)

        result = lax.map(run_group, (queries, list_groups))
        return result.reshape(TOKENS, HEAD_DIM)

    heads_out = lax.map(one_head, jnp.arange(HEADS, dtype=jnp.int32))
    return jnp.transpose(heads_out, (1, 0, 2)).reshape(TOKENS, HEADS * HEAD_DIM)
```

```python
import functools

import jax
import jax.numpy as jnp
from jax import lax
from jax.experimental import pallas as pl
from jax.experimental.pallas import tpu as pltpu
from jax.sharding import PartitionSpec as P

HEAD_DIM = 64
LANES = 128
MESH = pl.DeviceIdType.MESH
SCORE_SCALE = HEAD_DIM ** -0.5
AHEAD = 2


def flip(me, mask, count):
    total, weight = 0, 1
    while weight < count:
        bit = lax.rem(lax.div(me, weight) + lax.div(mask, weight), 2)
        total = total + bit * weight
        weight *= 2
    return total


def attend_tile(list_ref, tile, first, query, wins, stage, head, scores):
    listed = list_ref.shape[1]
    lane = lax.broadcasted_iota(jnp.int32, query.shape, 1)
    moved = pltpu.roll(query.astype(jnp.float32), HEAD_DIM, 1) * SCORE_SCALE
    keep = lane >= HEAD_DIM if head == 0 else lane < HEAD_DIM
    moved = jnp.where(keep, moved, 0.0).astype(jnp.bfloat16)
    values_low = head == 0
    top = None
    for j in range(listed):
        index = jnp.clip(list_ref[tile, j] - first, 0, wins[stage].shape[0] - 1)
        keys = wins[stage][index, :, 0:LANES]
        part = lax.dot_general(
            moved, keys, (((1,), (1,)), ((), ())), preferred_element_type=jnp.float32
        )
        scores[j] = part
        for c in range(0, part.shape[1], LANES):
            piece = part[:, c:c + LANES]
            top = piece if top is None else jnp.maximum(top, piece)
    row_max = jnp.max(top, axis=1, keepdims=True)
    total = None
    for j in range(listed):
        index = jnp.clip(list_ref[tile, j] - first, 0, wins[stage].shape[0] - 1)
        weights = jnp.exp(scores[j] - row_max).astype(jnp.bfloat16)
        if head == 0:
            values = wins[stage][index, :, LANES:2 * LANES]
        else:
            values = wins[stage][index, :, 0:LANES]
        value_lane = lax.broadcasted_iota(jnp.int32, values.shape, 1)
        ones = value_lane >= HEAD_DIM if values_low else value_lane < HEAD_DIM
        values = jnp.where(ones, jnp.ones_like(values), values)
        part = lax.dot_general(
            weights, values, (((1,), (0,)), ((), ())), preferred_element_type=jnp.float32
        )
        total = part if total is None else total + part
    return total / pltpu.roll(total, HEAD_DIM, 1)


def kernel(ulys, blks, units, stages, unit_width, list_ref, qkv_ref, out_ref, *scratch):
    count = len(stages)
    wins = scratch[:count]
    outs = scratch[count:count + units]
    (scores, own_sem, in_send, in_recv, halo_send, halo_recv,
     out_own, out_send, out_recv) = scratch[count + units:]
    me = lax.axis_index("uly")
    blk = lax.axis_index("blk")
    first = (blk - 1) * ulys
    has_prev = blk > 0
    has_next = blk < blks - 1

    def peer(step):
        return flip(me, ulys - 1 - step, ulys)

    def columns(owner, stage):
        unit, _, begin, width = stages[stage]
        start = (owner * units + unit) * unit_width + begin
        return qkv_ref.at[:, pl.ds(pl.multiple_of(start, LANES), width)]

    def inbound(stage, other):
        return pltpu.make_async_remote_copy(
            src_ref=columns(other, stage),
            dst_ref=wins[stage].at[ulys + me],
            send_sem=in_send.at[stage, other],
            recv_sem=in_recv.at[stage, me],
            device_id={"uly": other},
            device_id_type=MESH,
        )

    def arrival(stage, other):
        return pltpu.make_async_remote_copy(
            src_ref=columns(other, stage),
            dst_ref=wins[stage].at[ulys + other],
            send_sem=in_send.at[stage, other],
            recv_sem=in_recv.at[stage, other],
            device_id={"uly": other},
            device_id_type=MESH,
        )

    def own(stage):
        return pltpu.make_async_copy(
            columns(me, stage), wins[stage].at[ulys + me], own_sem.at[stage]
        )

    def halo(stage, side, tile):
        return pltpu.make_async_remote_copy(
            src_ref=wins[stage].at[ulys + tile],
            dst_ref=wins[stage].at[2 * ulys * side + tile],
            send_sem=halo_send.at[stage, side, tile],
            recv_sem=halo_recv.at[stage, side, tile],
            device_id={"blk": blk + 1 - 2 * side},
            device_id_type=MESH,
        )

    def out_columns(owner, unit):
        start = (owner * units + unit) * LANES
        return out_ref.at[:, pl.ds(pl.multiple_of(start, LANES), LANES)]

    def outbound(unit, other):
        return pltpu.make_async_remote_copy(
            src_ref=outs[unit].at[other],
            dst_ref=out_columns(me, unit),
            send_sem=out_send.at[unit, other],
            recv_sem=out_recv.at[unit, me],
            device_id={"uly": other},
            device_id_type=MESH,
        )

    def returned(unit, other):
        return pltpu.make_async_remote_copy(
            src_ref=outs[unit].at[other],
            dst_ref=out_columns(other, unit),
            send_sem=out_send.at[unit, other],
            recv_sem=out_recv.at[unit, other],
            device_id={"uly": other},
            device_id_type=MESH,
        )

    def out_here(unit):
        return pltpu.make_async_copy(
            outs[unit].at[me], out_columns(me, unit), out_own.at[unit]
        )

    def forward(stage, tile):
        @pl.when(has_next)
        def _():
            halo(stage, 0, tile).start()

        @pl.when(has_prev)
        def _():
            halo(stage, 1, tile).start()

    def steps(limit, body):
        def run(step, carry):
            body(step)
            return carry
        lax.fori_loop(0, limit, run, 0)

    barrier = pltpu.get_barrier_semaphore()

    def greet(step):
        pl.semaphore_signal(
            barrier, inc=1, device_id={"uly": peer(step)}, device_id_type=MESH
        )

    steps(ulys - 1, greet)

    @pl.when(has_next)
    def _():
        pl.semaphore_signal(barrier, inc=1, device_id={"blk": blk + 1}, device_id_type=MESH)

    @pl.when(has_prev)
    def _():
        pl.semaphore_signal(barrier, inc=1, device_id={"blk": blk - 1}, device_id_type=MESH)

    beside = jnp.where(has_prev, 1, 0) + jnp.where(has_next, 1, 0)
    pl.semaphore_wait(barrier, ulys - 1 + beside)

    for stage in range(min(AHEAD, count)):
        steps(ulys - 1, lambda step, stage=stage: inbound(stage, peer(step)).start())
    for stage in range(count):
        own(stage).start()

    def compute(stage, tile):
        unit, head, _, _ = stages[stage]
        if head == 0:
            query = wins[stage][ulys + tile, :, 0:LANES]
        else:
            query = wins[stage - 1][ulys + tile, :, LANES:2 * LANES]
        result = attend_tile(list_ref, tile, first, query, wins, stage, head, scores)
        lane = lax.broadcasted_iota(jnp.int32, result.shape, 1)
        if head == 0:
            outs[unit][tile] = jnp.where(lane < HEAD_DIM, result, 0.0).astype(jnp.bfloat16)
        else:
            before = outs[unit][tile].astype(jnp.float32)
            outs[unit][tile] = jnp.where(lane < HEAD_DIM, before, result).astype(jnp.bfloat16)

    for turn in range(count + 1):
        done = turn - 1
        if turn < count:
            own(turn).wait()
            forward(turn, me)
        if done >= 0:
            def arrived(tile, done=done):
                @pl.when(has_prev)
                def _():
                    halo(done, 0, tile).wait_recv()

                @pl.when(has_next)
                def _():
                    halo(done, 1, tile).wait_recv()

            steps(ulys, arrived)

        def body(step, turn=turn, done=done):
            other = peer(step)
            if turn < count:
                @pl.when(step < ulys - 1)
                def _():
                    arrival(turn, other).wait_recv()
                    forward(turn, other)
                    if turn + AHEAD < count:
                        inbound(turn + AHEAD, other).start()
            if done >= 0:
                compute(done, other)
                unit = stages[done][0]
                if done == count - 1 or stages[done + 1][0] != unit:
                    @pl.when(step < ulys - 1)
                    def _():
                        outbound(unit, other).start()

                    @pl.when(step == ulys - 1)
                    def _():
                        out_here(unit).start()

        steps(ulys, body)

    def finish(step):
        other = peer(step)
        for stage in range(count):
            inbound(stage, other).wait_send()
        for unit in range(units):
            outbound(unit, other).wait_send()
            returned(unit, other).wait_recv()

    steps(ulys - 1, finish)

    def finish_halo(tile):
        for stage in range(count):
            @pl.when(has_next)
            def _():
                halo(stage, 0, tile).wait_send()

            @pl.when(has_prev)
            def _():
                halo(stage, 1, tile).wait_send()

    steps(ulys, finish_halo)
    for unit in range(units):
        out_here(unit).wait()


def on_device(qkv, tile_list):
    tokens, width = qkv.shape
    ulys, blks = lax.axis_size("uly"), lax.axis_size("blk")
    heads = width // (3 * HEAD_DIM)
    heads_here = heads // ulys
    paired = heads_here % 2 == 0
    if paired:
        units, unit_width = heads_here // 2, 6 * HEAD_DIM
        stages = []
        for unit in range(units):
            stages += [(unit, 0, 0, 2 * LANES), (unit, 1, 2 * LANES, LANES)]
    else:
        units, unit_width = heads_here, 4 * HEAD_DIM
        stages = [(unit, 0, 0, 2 * LANES) for unit in range(units)]
        qkv = jnp.pad(
            qkv.reshape(tokens, heads, 3 * HEAD_DIM), ((0, 0), (0, 0), (0, HEAD_DIM))
        ).reshape(tokens, heads * unit_width)
    listed = tile_list.shape[1]
    count = len(stages)
    out_width = ulys * units * LANES
    dma = pltpu.SemaphoreType.DMA
    pairs = ulys * listed * heads_here
    out = pl.pallas_call(
        functools.partial(kernel, ulys, blks, units, tuple(stages), unit_width),
        out_shape=jax.ShapeDtypeStruct((tokens, out_width), jnp.bfloat16),
        in_specs=[
            pl.BlockSpec(memory_space=pltpu.SMEM),
            pl.BlockSpec(memory_space=pl.ANY),
        ],
        out_specs=pl.BlockSpec(memory_space=pl.ANY),
        scratch_shapes=[
            pltpu.VMEM((3 * ulys, tokens, stage[3]), jnp.bfloat16) for stage in stages
        ] + [
            pltpu.VMEM((ulys, tokens, LANES), jnp.bfloat16) for _ in range(units)
        ] + [
            pltpu.VMEM((listed, tokens, tokens), jnp.float32),
            dma((count,)),
            dma((count, ulys)),
            dma((count, ulys)),
            dma((count, 2, ulys)),
            dma((count, 2, ulys)),
            dma((units,)),
            dma((units, ulys)),
            dma((units, ulys)),
        ],
        compiler_params=pltpu.CompilerParams(
            collective_id=0, has_side_effects=True, vmem_limit_bytes=48 * 1024 * 1024
        ),
        cost_estimate=pl.CostEstimate(
            flops=4 * pairs * tokens * tokens * HEAD_DIM,
            bytes_accessed=2 * qkv.size * 2,
            transcendentals=pairs * tokens * tokens,
        ),
    )(tile_list, qkv)
    if not paired:
        out = out.reshape(tokens, heads, LANES)[:, :, :HEAD_DIM]
        out = out.reshape(tokens, heads * HEAD_DIM)
    return out


def solution(mesh):
    in_specs = (P(("blk", "uly"), None), P("blk", None))
    out_specs = P(("blk", "uly"), None)
    return jax.shard_map(
        on_device, mesh=mesh, in_specs=in_specs, out_specs=out_specs, check_vma=False
    )
```

```python
import functools

import jax
import jax.numpy as jnp
from jax import lax
from jax.experimental import pallas as pl
from jax.experimental.pallas import tpu as pltpu
from jax.sharding import PartitionSpec as P

HEAD_DIM = 64
LANES = 128
MESH = pl.DeviceIdType.MESH
SCORE_SCALE = HEAD_DIM ** -0.5
AHEAD = 4


def flip(me, mask, count):
    total, weight = 0, 1
    while weight < count:
        bit = lax.rem(lax.div(me, weight) + lax.div(mask, weight), 2)
        total = total + bit * weight
        weight *= 2
    return total


def attend_tile(list_ref, tile, first, query, wins, stage, head, scores):
    listed = list_ref.shape[1]
    lane = lax.broadcasted_iota(jnp.int32, query.shape, 1)
    moved = pltpu.roll(query.astype(jnp.float32), HEAD_DIM, 1) * SCORE_SCALE
    keep = lane >= HEAD_DIM if head == 0 else lane < HEAD_DIM
    moved = jnp.where(keep, moved, 0.0).astype(jnp.bfloat16)
    values_low = head == 0
    top = None
    for j in range(listed):
        index = jnp.clip(list_ref[tile, j] - first, 0, wins[stage].shape[0] - 1)
        keys = wins[stage][index, :, 0:LANES]
        part = lax.dot_general(
            moved, keys, (((1,), (1,)), ((), ())), preferred_element_type=jnp.float32
        )
        scores[j] = part
        for c in range(0, part.shape[1], LANES):
            piece = part[:, c:c + LANES]
            top = piece if top is None else jnp.maximum(top, piece)
    row_max = jnp.max(top, axis=1, keepdims=True)
    total = None
    for j in range(listed):
        index = jnp.clip(list_ref[tile, j] - first, 0, wins[stage].shape[0] - 1)
        weights = jnp.exp(scores[j] - row_max).astype(jnp.bfloat16)
        if head == 0:
            values = wins[stage][index, :, LANES:2 * LANES]
        else:
            values = wins[stage][index, :, 0:LANES]
        value_lane = lax.broadcasted_iota(jnp.int32, values.shape, 1)
        ones = value_lane >= HEAD_DIM if values_low else value_lane < HEAD_DIM
        values = jnp.where(ones, jnp.ones_like(values), values)
        part = lax.dot_general(
            weights, values, (((1,), (0,)), ((), ())), preferred_element_type=jnp.float32
        )
        total = part if total is None else total + part
    return total / pltpu.roll(total, HEAD_DIM, 1)


def kernel(ulys, blks, units, stages, unit_width, list_hbm, qkv_ref, out_ref, *scratch):
    count = len(stages)
    wins = scratch[:count]
    outs = scratch[count:count + units]
    (scores, list_ref, list_sem, own_sem, in_send, in_recv, halo_send, halo_recv,
     out_own, out_send, out_recv) = scratch[count + units:]
    list_copy = pltpu.make_async_copy(list_hbm, list_ref, list_sem)
    list_copy.start()
    me = lax.axis_index("uly")
    blk = lax.axis_index("blk")
    first = (blk - 1) * ulys
    has_prev = blk > 0
    has_next = blk < blks - 1

    def peer(step):
        return flip(me, ulys - 1 - step, ulys)

    def mixed(step):
        half, odd = lax.div(step, 2), lax.rem(step, 2)
        return flip(me, odd * (half + 1) + (1 - odd) * (ulys - 1 - half), ulys)

    def near(step):
        return flip(me, step + 1, ulys)

    def columns(owner, stage):
        unit, _, begin, width = stages[stage]
        start = (owner * units + unit) * unit_width + begin
        return qkv_ref.at[:, pl.ds(pl.multiple_of(start, LANES), width)]

    def inbound(stage, other):
        return pltpu.make_async_remote_copy(
            src_ref=columns(other, stage),
            dst_ref=wins[stage].at[ulys + me],
            send_sem=in_send.at[stage, other],
            recv_sem=in_recv.at[stage, me],
            device_id={"uly": other},
            device_id_type=MESH,
        )

    def arrival(stage, other):
        return pltpu.make_async_remote_copy(
            src_ref=columns(other, stage),
            dst_ref=wins[stage].at[ulys + other],
            send_sem=in_send.at[stage, other],
            recv_sem=in_recv.at[stage, other],
            device_id={"uly": other},
            device_id_type=MESH,
        )

    def own(stage):
        return pltpu.make_async_copy(
            columns(me, stage), wins[stage].at[ulys + me], own_sem.at[stage]
        )

    def halo(stage, side, tile):
        return pltpu.make_async_remote_copy(
            src_ref=wins[stage].at[ulys + tile],
            dst_ref=wins[stage].at[2 * ulys * side + tile],
            send_sem=halo_send.at[stage, side, tile],
            recv_sem=halo_recv.at[stage, side, tile],
            device_id={"blk": blk + 1 - 2 * side},
            device_id_type=MESH,
        )

    def out_columns(owner, unit):
        start = (owner * units + unit) * LANES
        return out_ref.at[:, pl.ds(pl.multiple_of(start, LANES), LANES)]

    def outbound(unit, other):
        return pltpu.make_async_remote_copy(
            src_ref=outs[unit].at[other],
            dst_ref=out_columns(me, unit),
            send_sem=out_send.at[unit, other],
            recv_sem=out_recv.at[unit, me],
            device_id={"uly": other},
            device_id_type=MESH,
        )

    def returned(unit, other):
        return pltpu.make_async_remote_copy(
            src_ref=outs[unit].at[other],
            dst_ref=out_columns(other, unit),
            send_sem=out_send.at[unit, other],
            recv_sem=out_recv.at[unit, other],
            device_id={"uly": other},
            device_id_type=MESH,
        )

    def out_here(unit):
        return pltpu.make_async_copy(
            outs[unit].at[me], out_columns(me, unit), out_own.at[unit]
        )

    def forward(stage, tile):
        @pl.when(has_next)
        def _():
            halo(stage, 0, tile).start()

        @pl.when(has_prev)
        def _():
            halo(stage, 1, tile).start()

    def steps(limit, body):
        def run(step, carry):
            body(step)
            return carry
        lax.fori_loop(0, limit, run, 0)

    barrier = pltpu.get_barrier_semaphore()

    def greet(step):
        pl.semaphore_signal(
            barrier, inc=1, device_id={"uly": peer(step)}, device_id_type=MESH
        )

    steps(ulys - 1, greet)

    @pl.when(has_next)
    def _():
        pl.semaphore_signal(barrier, inc=1, device_id={"blk": blk + 1}, device_id_type=MESH)

    @pl.when(has_prev)
    def _():
        pl.semaphore_signal(barrier, inc=1, device_id={"blk": blk - 1}, device_id_type=MESH)

    beside = jnp.where(has_prev, 1, 0) + jnp.where(has_next, 1, 0)
    pl.semaphore_wait(barrier, ulys - 1 + beside)

    for stage in range(min(AHEAD, count)):
        steps(ulys - 1, lambda step, stage=stage: inbound(stage, mixed(step)).start())
    for stage in range(count):
        own(stage).start()

    def compute(stage, tile):
        unit, head, _, _ = stages[stage]
        if head == 0:
            query = wins[stage][ulys + tile, :, 0:LANES]
        else:
            query = wins[stage - 1][ulys + tile, :, LANES:2 * LANES]
        result = attend_tile(list_ref, tile, first, query, wins, stage, head, scores)
        lane = lax.broadcasted_iota(jnp.int32, result.shape, 1)
        if head == 0:
            outs[unit][tile] = jnp.where(lane < HEAD_DIM, result, 0.0).astype(jnp.bfloat16)
        else:
            before = outs[unit][tile].astype(jnp.float32)
            outs[unit][tile] = jnp.where(lane < HEAD_DIM, before, result).astype(jnp.bfloat16)

    list_copy.wait()
    for turn in range(count + 1):
        done = turn - 1
        if turn < count:
            own(turn).wait()
            forward(turn, me)
        if done >= 0:
            def arrived(tile, done=done):
                @pl.when(has_prev)
                def _():
                    halo(done, 0, tile).wait_recv()

                @pl.when(has_next)
                def _():
                    halo(done, 1, tile).wait_recv()

            steps(ulys, arrived)

        def body(step, turn=turn, done=done):
            other = peer(step)
            if turn < count:
                @pl.when(step < ulys - 1)
                def _():
                    source = near(step)
                    arrival(turn, source).wait_recv()
                    forward(turn, source)
                    if turn + AHEAD < count:
                        inbound(turn + AHEAD, source).start()
            if done >= 0:
                compute(done, other)
                unit = stages[done][0]
                if done == count - 1 or stages[done + 1][0] != unit:
                    @pl.when(step < ulys - 1)
                    def _():
                        outbound(unit, other).start()

                    @pl.when(step == ulys - 1)
                    def _():
                        out_here(unit).start()

        steps(ulys, body)

    def finish(step):
        other = peer(step)
        for stage in range(count):
            inbound(stage, other).wait_send()
        for unit in range(units):
            outbound(unit, other).wait_send()
            returned(unit, other).wait_recv()

    steps(ulys - 1, finish)

    def finish_halo(tile):
        for stage in range(count):
            @pl.when(has_next)
            def _():
                halo(stage, 0, tile).wait_send()

            @pl.when(has_prev)
            def _():
                halo(stage, 1, tile).wait_send()

    steps(ulys, finish_halo)
    for unit in range(units):
        out_here(unit).wait()


def on_device(qkv, tile_list):
    tokens, width = qkv.shape
    ulys, blks = lax.axis_size("uly"), lax.axis_size("blk")
    heads = width // (3 * HEAD_DIM)
    heads_here = heads // ulys
    paired = heads_here % 2 == 0
    if paired:
        units, unit_width = heads_here // 2, 6 * HEAD_DIM
        stages = []
        for unit in range(units):
            stages += [(unit, 0, 0, 2 * LANES), (unit, 1, 2 * LANES, LANES)]
    else:
        units, unit_width = heads_here, 4 * HEAD_DIM
        stages = [(unit, 0, 0, 2 * LANES) for unit in range(units)]
        qkv = jnp.pad(
            qkv.reshape(tokens, heads, 3 * HEAD_DIM), ((0, 0), (0, 0), (0, HEAD_DIM))
        ).reshape(tokens, heads * unit_width)
    listed = tile_list.shape[1]
    count = len(stages)
    out_width = ulys * units * LANES
    dma = pltpu.SemaphoreType.DMA
    pairs = ulys * listed * heads_here
    out = pl.pallas_call(
        functools.partial(kernel, ulys, blks, units, tuple(stages), unit_width),
        out_shape=jax.ShapeDtypeStruct((tokens, out_width), jnp.bfloat16),
        in_specs=[
            pl.BlockSpec(memory_space=pltpu.HBM),
            pl.BlockSpec(memory_space=pltpu.HBM),
        ],
        out_specs=pl.BlockSpec(memory_space=pl.ANY),
        scratch_shapes=[
            pltpu.VMEM((3 * ulys, tokens, stage[3]), jnp.bfloat16) for stage in stages
        ] + [
            pltpu.VMEM((ulys, tokens, LANES), jnp.bfloat16) for _ in range(units)
        ] + [
            pltpu.VMEM((listed, tokens, tokens), jnp.float32),
            pltpu.SMEM(tile_list.shape, jnp.int32),
            dma(()),
            dma((count,)),
            dma((count, ulys)),
            dma((count, ulys)),
            dma((count, 2, ulys)),
            dma((count, 2, ulys)),
            dma((units,)),
            dma((units, ulys)),
            dma((units, ulys)),
        ],
        compiler_params=pltpu.CompilerParams(
            collective_id=0, has_side_effects=True, vmem_limit_bytes=63 * 1024 * 1024
        ),
        cost_estimate=pl.CostEstimate(
            flops=4 * pairs * tokens * tokens * HEAD_DIM,
            bytes_accessed=2 * qkv.size * 2,
            transcendentals=pairs * tokens * tokens,
        ),
    )(tile_list, qkv)
    if not paired:
        out = out.reshape(tokens, heads, LANES)[:, :, :HEAD_DIM]
        out = out.reshape(tokens, heads * HEAD_DIM)
    return out


def solution(mesh):
    in_specs = (P(("blk", "uly"), None), P("blk", None))
    out_specs = P(("blk", "uly"), None)
    return jax.shard_map(
        on_device, mesh=mesh, in_specs=in_specs, out_specs=out_specs, check_vma=False
    )
```

```python
import functools

import jax
import jax.numpy as jnp
from jax import lax
from jax.experimental import pallas as pl
from jax.experimental.pallas import tpu as pltpu
from jax.sharding import PartitionSpec as P

HEAD_DIM = 64
LANES = 128
MESH = pl.DeviceIdType.MESH
SCORE_SCALE = HEAD_DIM ** -0.5
AHEAD = 4
ONES = 16


def flip(me, mask, count):
    total, weight = 0, 1
    while weight < count:
        bit = lax.rem(lax.div(me, weight) + lax.div(mask, weight), 2)
        total = total + bit * weight
        weight *= 2
    return total


def attend_tile(list_ref, tile, first, query, window, turned, head, scores):
    listed = list_ref.shape[1]
    last = window.shape[0] - 1
    across = jnp.transpose(query)
    blank = jnp.zeros((HEAD_DIM, across.shape[1]), jnp.bfloat16)
    if head == 0:
        part = across[:HEAD_DIM].astype(jnp.float32) * SCORE_SCALE
        across = jnp.concatenate([blank, part.astype(jnp.bfloat16)], axis=0)
    else:
        part = across[HEAD_DIM:].astype(jnp.float32) * SCORE_SCALE
        across = jnp.concatenate([part.astype(jnp.bfloat16), blank], axis=0)
    top = None
    for j in range(listed):
        index = jnp.clip(list_ref[tile, j] - first, 0, last)
        keys = window[index, :, 0:LANES]
        part = jnp.dot(keys, across, preferred_element_type=jnp.float32)
        scores[j] = part
        piece = jnp.max(part.reshape(part.shape[0] // 8, 8, part.shape[1]), axis=0)
        top = piece if top is None else jnp.maximum(top, piece)
    col_max = jnp.max(top, axis=0, keepdims=True)
    total = None
    for j in range(listed):
        index = jnp.clip(list_ref[tile, j] - first, 0, last)
        weights = jnp.exp(scores[j] - col_max).astype(jnp.bfloat16)
        part = jnp.dot(turned[index], weights, preferred_element_type=jnp.float32)
        total = part if total is None else total + part
    return total[:HEAD_DIM] / total[HEAD_DIM:HEAD_DIM + 1]


def kernel(ulys, blks, units, stages, unit_width, list_hbm, qkv_ref, out_ref, *scratch):
    count = len(stages)
    wins = scratch[:count]
    outs = scratch[count:count + units]
    (scores, turned, half, list_ref, list_sem, own_sem, in_send, in_recv, halo_send, halo_recv,
     out_own, out_send, out_recv) = scratch[count + units:]
    list_copy = pltpu.make_async_copy(list_hbm, list_ref, list_sem)
    list_copy.start()
    me = lax.axis_index("uly")
    blk = lax.axis_index("blk")
    first = (blk - 1) * ulys
    has_prev = blk > 0
    has_next = blk < blks - 1

    def peer(step):
        return flip(me, ulys - 1 - step, ulys)

    def mixed(step):
        half, odd = lax.div(step, 2), lax.rem(step, 2)
        return flip(me, odd * (half + 1) + (1 - odd) * (ulys - 1 - half), ulys)

    def near(step):
        return flip(me, step + 1, ulys)

    def columns(owner, stage):
        unit, _, begin, width = stages[stage]
        start = (owner * units + unit) * unit_width + begin
        return qkv_ref.at[:, pl.ds(pl.multiple_of(start, LANES), width)]

    def inbound(stage, other):
        return pltpu.make_async_remote_copy(
            src_ref=columns(other, stage),
            dst_ref=wins[stage].at[ulys + me],
            send_sem=in_send.at[stage, other],
            recv_sem=in_recv.at[stage, me],
            device_id={"uly": other},
            device_id_type=MESH,
        )

    def arrival(stage, other):
        return pltpu.make_async_remote_copy(
            src_ref=columns(other, stage),
            dst_ref=wins[stage].at[ulys + other],
            send_sem=in_send.at[stage, other],
            recv_sem=in_recv.at[stage, other],
            device_id={"uly": other},
            device_id_type=MESH,
        )

    def own(stage):
        return pltpu.make_async_copy(
            columns(me, stage), wins[stage].at[ulys + me], own_sem.at[stage]
        )

    def halo(stage, side, tile):
        return pltpu.make_async_remote_copy(
            src_ref=wins[stage].at[ulys + tile],
            dst_ref=wins[stage].at[2 * ulys * side + tile],
            send_sem=halo_send.at[stage, side, tile],
            recv_sem=halo_recv.at[stage, side, tile],
            device_id={"blk": blk + 1 - 2 * side},
            device_id_type=MESH,
        )

    def out_columns(owner, unit):
        start = (owner * units + unit) * LANES
        return out_ref.at[:, pl.ds(pl.multiple_of(start, LANES), LANES)]

    def outbound(unit, other):
        return pltpu.make_async_remote_copy(
            src_ref=outs[unit].at[other],
            dst_ref=out_columns(me, unit),
            send_sem=out_send.at[unit, other],
            recv_sem=out_recv.at[unit, me],
            device_id={"uly": other},
            device_id_type=MESH,
        )

    def returned(unit, other):
        return pltpu.make_async_remote_copy(
            src_ref=outs[unit].at[other],
            dst_ref=out_columns(other, unit),
            send_sem=out_send.at[unit, other],
            recv_sem=out_recv.at[unit, other],
            device_id={"uly": other},
            device_id_type=MESH,
        )

    def out_here(unit):
        return pltpu.make_async_copy(
            outs[unit].at[me], out_columns(me, unit), out_own.at[unit]
        )

    def forward(stage, tile):
        @pl.when(has_next)
        def _():
            halo(stage, 0, tile).start()

        @pl.when(has_prev)
        def _():
            halo(stage, 1, tile).start()

    def steps(limit, body):
        def run(step, carry):
            body(step)
            return carry
        lax.fori_loop(0, limit, run, 0)

    barrier = pltpu.get_barrier_semaphore()

    def greet(step):
        pl.semaphore_signal(
            barrier, inc=1, device_id={"uly": peer(step)}, device_id_type=MESH
        )

    steps(ulys - 1, greet)

    @pl.when(has_next)
    def _():
        pl.semaphore_signal(barrier, inc=1, device_id={"blk": blk + 1}, device_id_type=MESH)

    @pl.when(has_prev)
    def _():
        pl.semaphore_signal(barrier, inc=1, device_id={"blk": blk - 1}, device_id_type=MESH)

    beside = jnp.where(has_prev, 1, 0) + jnp.where(has_next, 1, 0)
    pl.semaphore_wait(barrier, ulys - 1 + beside)

    for stage in range(min(AHEAD, count)):
        steps(ulys - 1, lambda step, stage=stage: inbound(stage, mixed(step)).start())
    for stage in range(count):
        own(stage).start()

    def compute(stage, tile):
        unit, head, _, _ = stages[stage]
        if head == 0:
            query = wins[stage][ulys + tile, :, 0:LANES]
        else:
            query = wins[stage - 1][ulys + tile, :, LANES:2 * LANES]
        result = attend_tile(
            list_ref, tile, first, query, wins[stage], turned, head, scores
        ).astype(jnp.bfloat16)
        if head == 0:
            half[tile] = result
        if closes(stage):
            low = half[tile] if head == 1 else result
            high = result if head == 1 else jnp.zeros_like(result)
            outs[unit][tile] = jnp.transpose(jnp.concatenate([low, high], axis=0))

    def closes(stage):
        return stage == count - 1 or stages[stage + 1][0] != stages[stage][0]

    def turn_values(stage, index):
        head = stages[stage][1]
        if head == 0:
            values = jnp.transpose(wins[stage][index, :, LANES:2 * LANES])[:HEAD_DIM]
        else:
            values = jnp.transpose(wins[stage][index, :, 0:LANES])[HEAD_DIM:]
        ones = jnp.ones((ONES, values.shape[1]), jnp.bfloat16)
        turned[index] = jnp.concatenate([values, ones], axis=0)

    list_copy.wait()
    for turn in range(count + 1):
        done = turn - 1
        if turn < count:
            own(turn).wait()
            forward(turn, me)
        if done >= 0:
            def arrived(tile, done=done):
                @pl.when(has_prev)
                def _():
                    halo(done, 0, tile).wait_recv()

                @pl.when(has_next)
                def _():
                    halo(done, 1, tile).wait_recv()

            steps(ulys, arrived)
            low = jnp.where(has_prev, 0, ulys)
            high = jnp.where(has_next, 3 * ulys, 2 * ulys)

            def turn_one(index, carry, done=done):
                turn_values(done, index)
                return carry

            lax.fori_loop(low, high, turn_one, 0)

        def body(step, turn=turn, done=done):
            other = peer(step)
            if turn < count:
                @pl.when(step < ulys - 1)
                def _():
                    source = near(step)
                    arrival(turn, source).wait_recv()
                    forward(turn, source)
                    if turn + AHEAD < count:
                        inbound(turn + AHEAD, source).start()
            if done >= 0:
                compute(done, other)
                unit = stages[done][0]
                if closes(done):
                    @pl.when(step < ulys - 1)
                    def _():
                        outbound(unit, other).start()

                    @pl.when(step == ulys - 1)
                    def _():
                        out_here(unit).start()

        steps(ulys, body)

    def finish(step):
        other = peer(step)
        for stage in range(count):
            inbound(stage, other).wait_send()
        for unit in range(units):
            outbound(unit, other).wait_send()
            returned(unit, other).wait_recv()

    steps(ulys - 1, finish)

    def finish_halo(tile):
        for stage in range(count):
            @pl.when(has_next)
            def _():
                halo(stage, 0, tile).wait_send()

            @pl.when(has_prev)
            def _():
                halo(stage, 1, tile).wait_send()

    steps(ulys, finish_halo)
    for unit in range(units):
        out_here(unit).wait()


def on_device(qkv, tile_list):
    tokens, width = qkv.shape
    ulys, blks = lax.axis_size("uly"), lax.axis_size("blk")
    heads = width // (3 * HEAD_DIM)
    heads_here = heads // ulys
    paired = heads_here % 2 == 0
    if paired:
        units, unit_width = heads_here // 2, 6 * HEAD_DIM
        stages = []
        for unit in range(units):
            stages += [(unit, 0, 0, 2 * LANES), (unit, 1, 2 * LANES, LANES)]
    else:
        units, unit_width = heads_here, 4 * HEAD_DIM
        stages = [(unit, 0, 0, 2 * LANES) for unit in range(units)]
        qkv = jnp.pad(
            qkv.reshape(tokens, heads, 3 * HEAD_DIM), ((0, 0), (0, 0), (0, HEAD_DIM))
        ).reshape(tokens, heads * unit_width)
    listed = tile_list.shape[1]
    count = len(stages)
    out_width = ulys * units * LANES
    dma = pltpu.SemaphoreType.DMA
    pairs = ulys * listed * heads_here
    out = pl.pallas_call(
        functools.partial(kernel, ulys, blks, units, tuple(stages), unit_width),
        out_shape=jax.ShapeDtypeStruct((tokens, out_width), jnp.bfloat16),
        in_specs=[
            pl.BlockSpec(memory_space=pltpu.HBM),
            pl.BlockSpec(memory_space=pltpu.HBM),
        ],
        out_specs=pl.BlockSpec(memory_space=pl.ANY),
        scratch_shapes=[
            pltpu.VMEM((3 * ulys, tokens, stage[3]), jnp.bfloat16) for stage in stages
        ] + [
            pltpu.VMEM((ulys, tokens, LANES), jnp.bfloat16) for _ in range(units)
        ] + [
            pltpu.VMEM((listed, tokens, tokens), jnp.float32),
            pltpu.VMEM((3 * ulys, HEAD_DIM + ONES, tokens), jnp.bfloat16),
            pltpu.VMEM((ulys, HEAD_DIM, tokens), jnp.bfloat16),
            pltpu.SMEM(tile_list.shape, jnp.int32),
            dma(()),
            dma((count,)),
            dma((count, ulys)),
            dma((count, ulys)),
            dma((count, 2, ulys)),
            dma((count, 2, ulys)),
            dma((units,)),
            dma((units, ulys)),
            dma((units, ulys)),
        ],
        compiler_params=pltpu.CompilerParams(
            collective_id=0, has_side_effects=True, vmem_limit_bytes=62 * 1024 * 1024
        ),
        cost_estimate=pl.CostEstimate(
            flops=4 * pairs * tokens * tokens * HEAD_DIM,
            bytes_accessed=2 * qkv.size * 2,
            transcendentals=pairs * tokens * tokens,
        ),
    )(tile_list, qkv)
    if not paired:
        out = out.reshape(tokens, heads, LANES)[:, :, :HEAD_DIM]
        out = out.reshape(tokens, heads * HEAD_DIM)
    return out


def solution(mesh):
    in_specs = (P(("blk", "uly"), None), P("blk", None))
    out_specs = P(("blk", "uly"), None)
    return jax.shard_map(
        on_device, mesh=mesh, in_specs=in_specs, out_specs=out_specs, check_vma=False
    )
```

```python
import functools

import jax
import jax.numpy as jnp
from jax import lax
from jax.experimental import pallas as pl
from jax.experimental.pallas import tpu as pltpu
from jax.sharding import PartitionSpec as P

HEAD_DIM = 64
LANES = 128
MESH = pl.DeviceIdType.MESH
SCORE_SCALE = HEAD_DIM ** -0.5
AHEAD = 4


def flip(me, mask, count):
    total, weight = 0, 1
    while weight < count:
        bit = lax.rem(lax.div(me, weight) + lax.div(mask, weight), 2)
        total = total + bit * weight
        weight *= 2
    return total


def attend_tile(list_ref, tile, first, query, wins, stage, head, scores):
    listed = list_ref.shape[1]
    lane = lax.broadcasted_iota(jnp.int32, query.shape, 1)
    moved = pltpu.roll(query.astype(jnp.float32), HEAD_DIM, 1) * SCORE_SCALE
    keep = lane >= HEAD_DIM if head == 0 else lane < HEAD_DIM
    moved = jnp.where(keep, moved, 0.0).astype(jnp.bfloat16)
    values_low = head == 0
    top = None
    for j in range(listed):
        index = jnp.clip(list_ref[tile, j] - first, 0, wins[stage].shape[0] - 1)
        keys = wins[stage][index, :, 0:LANES]
        part = lax.dot_general(
            moved, keys, (((1,), (1,)), ((), ())), preferred_element_type=jnp.float32
        )
        scores[j] = part
        for c in range(0, part.shape[1], LANES):
            piece = part[:, c:c + LANES]
            top = piece if top is None else jnp.maximum(top, piece)
    row_max = jnp.max(top, axis=1, keepdims=True)
    total = None
    for j in range(listed):
        index = jnp.clip(list_ref[tile, j] - first, 0, wins[stage].shape[0] - 1)
        weights = jnp.exp(scores[j] - row_max).astype(jnp.bfloat16)
        if head == 0:
            values = wins[stage][index, :, LANES:2 * LANES]
        else:
            values = wins[stage][index, :, 0:LANES]
        value_lane = lax.broadcasted_iota(jnp.int32, values.shape, 1)
        ones = value_lane >= HEAD_DIM if values_low else value_lane < HEAD_DIM
        values = jnp.where(ones, jnp.ones_like(values), values)
        part = lax.dot_general(
            weights, values, (((1,), (0,)), ((), ())), preferred_element_type=jnp.float32
        )
        total = part if total is None else total + part
    return total / pltpu.roll(total, HEAD_DIM, 1)


def kernel(ulys, blks, units, stages, unit_width, list_hbm, qkv_ref, out_ref, *scratch):
    count = len(stages)
    wins = scratch[:count]
    outs = scratch[count:count + units]
    (scores, list_ref, list_sem, own_sem, in_send, in_recv, halo_send, halo_recv,
     out_own, out_send, out_recv) = scratch[count + units:]
    list_copy = pltpu.make_async_copy(list_hbm, list_ref, list_sem)
    list_copy.start()
    me = lax.axis_index("uly")
    blk = lax.axis_index("blk")
    first = (blk - 1) * ulys
    has_prev = blk > 0
    has_next = blk < blks - 1

    def peer(step):
        return flip(me, ulys - 1 - step, ulys)

    def mixed(step):
        half, odd = lax.div(step, 2), lax.rem(step, 2)
        return flip(me, odd * (half + 1) + (1 - odd) * (ulys - 1 - half), ulys)

    def near(step):
        return flip(me, step + 1, ulys)

    def columns(owner, stage):
        unit, _, begin, width = stages[stage]
        start = (owner * units + unit) * unit_width + begin
        return qkv_ref.at[:, pl.ds(pl.multiple_of(start, LANES), width)]

    def inbound(stage, other):
        return pltpu.make_async_remote_copy(
            src_ref=columns(other, stage),
            dst_ref=wins[stage].at[ulys + me],
            send_sem=in_send.at[stage, other],
            recv_sem=in_recv.at[stage, me],
            device_id={"uly": other},
            device_id_type=MESH,
        )

    def arrival(stage, other):
        return pltpu.make_async_remote_copy(
            src_ref=columns(other, stage),
            dst_ref=wins[stage].at[ulys + other],
            send_sem=in_send.at[stage, other],
            recv_sem=in_recv.at[stage, other],
            device_id={"uly": other},
            device_id_type=MESH,
        )

    def own(stage):
        return pltpu.make_async_copy(
            columns(me, stage), wins[stage].at[ulys + me], own_sem.at[stage]
        )

    def halo(stage, side, tile):
        return pltpu.make_async_remote_copy(
            src_ref=wins[stage].at[ulys + tile],
            dst_ref=wins[stage].at[2 * ulys * side + tile],
            send_sem=halo_send.at[stage, side, tile],
            recv_sem=halo_recv.at[stage, side, tile],
            device_id={"blk": blk + 1 - 2 * side},
            device_id_type=MESH,
        )

    def out_columns(owner, unit):
        start = (owner * units + unit) * LANES
        return out_ref.at[:, pl.ds(pl.multiple_of(start, LANES), LANES)]

    def outbound(unit, other):
        return pltpu.make_async_remote_copy(
            src_ref=outs[unit].at[other],
            dst_ref=out_columns(me, unit),
            send_sem=out_send.at[unit, other],
            recv_sem=out_recv.at[unit, me],
            device_id={"uly": other},
            device_id_type=MESH,
        )

    def returned(unit, other):
        return pltpu.make_async_remote_copy(
            src_ref=outs[unit].at[other],
            dst_ref=out_columns(other, unit),
            send_sem=out_send.at[unit, other],
            recv_sem=out_recv.at[unit, other],
            device_id={"uly": other},
            device_id_type=MESH,
        )

    def out_here(unit):
        return pltpu.make_async_copy(
            outs[unit].at[me], out_columns(me, unit), out_own.at[unit]
        )

    def forward(stage, tile):
        @pl.when(has_next)
        def _():
            halo(stage, 0, tile).start()

        @pl.when(has_prev)
        def _():
            halo(stage, 1, tile).start()

    def steps(limit, body):
        def run(step, carry):
            body(step)
            return carry
        lax.fori_loop(0, limit, run, 0)

    barrier = pltpu.get_barrier_semaphore()

    def greet(step):
        pl.semaphore_signal(
            barrier, inc=1, device_id={"uly": peer(step)}, device_id_type=MESH
        )

    steps(ulys - 1, greet)

    @pl.when(has_next)
    def _():
        pl.semaphore_signal(barrier, inc=1, device_id={"blk": blk + 1}, device_id_type=MESH)

    @pl.when(has_prev)
    def _():
        pl.semaphore_signal(barrier, inc=1, device_id={"blk": blk - 1}, device_id_type=MESH)

    beside = jnp.where(has_prev, 1, 0) + jnp.where(has_next, 1, 0)
    pl.semaphore_wait(barrier, ulys - 1 + beside)

    for stage in range(min(AHEAD, count)):
        steps(ulys - 1, lambda step, stage=stage: inbound(stage, mixed(step)).start())
    for stage in range(count):
        own(stage).start()

    def compute(stage, tile):
        unit, head, _, _ = stages[stage]
        if head == 0:
            query = wins[stage][ulys + tile, :, 0:LANES]
        else:
            query = wins[stage - 1][ulys + tile, :, LANES:2 * LANES]
        result = attend_tile(list_ref, tile, first, query, wins, stage, head, scores)
        lane = lax.broadcasted_iota(jnp.int32, result.shape, 1)
        if head == 0:
            outs[unit][tile] = jnp.where(lane < HEAD_DIM, result, 0.0).astype(jnp.bfloat16)
        else:
            before = outs[unit][tile].astype(jnp.float32)
            outs[unit][tile] = jnp.where(lane < HEAD_DIM, before, result).astype(jnp.bfloat16)

    list_copy.wait()
    for turn in range(count + 1):
        done = turn - 1
        if turn < count:
            own(turn).wait()
            forward(turn, me)
        if done >= 0:
            def arrived(tile, done=done):
                @pl.when(has_prev)
                def _():
                    halo(done, 0, tile).wait_recv()

                @pl.when(has_next)
                def _():
                    halo(done, 1, tile).wait_recv()

            steps(ulys, arrived)

        def take(step, turn=turn):
            source = near(step)
            arrival(turn, source).wait_recv()
            forward(turn, source)

        def body(step, turn=turn, done=done):
            other = peer(step)
            if done >= 0:
                compute(done, other)
                unit = stages[done][0]
                if unit == units - 1 and done == count - 1:
                    @pl.when(step < ulys - 1)
                    def _():
                        outbound(unit, other).start()

                    @pl.when(step == ulys - 1)
                    def _():
                        out_here(unit).start()

            if turn < count:
                @pl.when(step < ulys // 2 - 1)
                def _():
                    take(step)

        steps(ulys, body)
        if turn < count:
            steps(ulys // 2, lambda step, take=take: take(step + ulys // 2 - 1))
        if turn == count - 1:
            def early(step):
                for unit in range(units - 1):
                    outbound(unit, peer(step)).start()

            steps(ulys - 1, early)
            for unit in range(units - 1):
                out_here(unit).start()

    def finish(step):
        other = peer(step)
        for stage in range(count):
            inbound(stage, other).wait_send()
        for unit in range(units):
            outbound(unit, other).wait_send()
            returned(unit, other).wait_recv()

    steps(ulys - 1, finish)

    def finish_halo(tile):
        for stage in range(count):
            @pl.when(has_next)
            def _():
                halo(stage, 0, tile).wait_send()

            @pl.when(has_prev)
            def _():
                halo(stage, 1, tile).wait_send()

    steps(ulys, finish_halo)
    for unit in range(units):
        out_here(unit).wait()


def on_device(qkv, tile_list):
    tokens, width = qkv.shape
    ulys, blks = lax.axis_size("uly"), lax.axis_size("blk")
    heads = width // (3 * HEAD_DIM)
    heads_here = heads // ulys
    paired = heads_here % 2 == 0
    if paired:
        units, unit_width = heads_here // 2, 6 * HEAD_DIM
        stages = []
        for unit in range(units):
            stages += [(unit, 0, 0, 2 * LANES), (unit, 1, 2 * LANES, LANES)]
    else:
        units, unit_width = heads_here, 4 * HEAD_DIM
        stages = [(unit, 0, 0, 2 * LANES) for unit in range(units)]
        qkv = jnp.pad(
            qkv.reshape(tokens, heads, 3 * HEAD_DIM), ((0, 0), (0, 0), (0, HEAD_DIM))
        ).reshape(tokens, heads * unit_width)
    listed = tile_list.shape[1]
    count = len(stages)
    out_width = ulys * units * LANES
    dma = pltpu.SemaphoreType.DMA
    pairs = ulys * listed * heads_here
    out = pl.pallas_call(
        functools.partial(kernel, ulys, blks, units, tuple(stages), unit_width),
        out_shape=jax.ShapeDtypeStruct((tokens, out_width), jnp.bfloat16),
        in_specs=[
            pl.BlockSpec(memory_space=pltpu.HBM),
            pl.BlockSpec(memory_space=pltpu.HBM),
        ],
        out_specs=pl.BlockSpec(memory_space=pl.ANY),
        scratch_shapes=[
            pltpu.VMEM((3 * ulys, tokens, stage[3]), jnp.bfloat16) for stage in stages
        ] + [
            pltpu.VMEM((ulys, tokens, LANES), jnp.bfloat16) for _ in range(units)
        ] + [
            pltpu.VMEM((listed, tokens, tokens), jnp.float32),
            pltpu.SMEM(tile_list.shape, jnp.int32),
            dma(()),
            dma((count,)),
            dma((count, ulys)),
            dma((count, ulys)),
            dma((count, 2, ulys)),
            dma((count, 2, ulys)),
            dma((units,)),
            dma((units, ulys)),
            dma((units, ulys)),
        ],
        compiler_params=pltpu.CompilerParams(
            collective_id=0, has_side_effects=True, vmem_limit_bytes=50 * 1024 * 1024
        ),
        cost_estimate=pl.CostEstimate(
            flops=4 * pairs * tokens * tokens * HEAD_DIM,
            bytes_accessed=2 * qkv.size * 2,
            transcendentals=pairs * tokens * tokens,
        ),
    )(tile_list, qkv)
    if not paired:
        out = out.reshape(tokens, heads, LANES)[:, :, :HEAD_DIM]
        out = out.reshape(tokens, heads * HEAD_DIM)
    return out


def solution(mesh):
    in_specs = (P(("blk", "uly"), None), P("blk", None))
    out_specs = P(("blk", "uly"), None)
    return jax.shard_map(
        on_device, mesh=mesh, in_specs=in_specs, out_specs=out_specs, check_vma=False
    )
```

```python
import functools

import jax
import jax.numpy as jnp
from jax import lax
from jax.experimental import pallas as pl
from jax.experimental.pallas import tpu as pltpu
from jax.sharding import PartitionSpec as P

HEAD_DIM = 64
LANES = 128
MESH = pl.DeviceIdType.MESH
SCORE_SCALE = HEAD_DIM ** -0.5
AHEAD = 4


def flip(me, mask, count):
    total, weight = 0, 1
    while weight < count:
        bit = lax.rem(lax.div(me, weight) + lax.div(mask, weight), 2)
        total = total + bit * weight
        weight *= 2
    return total


def attend_step(list_ref, first, window, value_at, head, now, later):
    listed = list_ref.shape[1]
    last = window.shape[0] - 1
    if later is not None:
        next_tile, query, next_scores, next_maxima = later
        lane = lax.broadcasted_iota(jnp.int32, query.shape, 1)
        moved = pltpu.roll(query.astype(jnp.float32), HEAD_DIM, 1) * SCORE_SCALE
        keep = lane >= HEAD_DIM if head == 0 else lane < HEAD_DIM
        moved = jnp.where(keep, moved, 0.0).astype(jnp.bfloat16)
    top = None
    total = None
    for j in range(listed):
        if later is not None:
            index = jnp.clip(list_ref[next_tile, j] - first, 0, last)
            keys = window[index, :, 0:LANES]
            part = lax.dot_general(
                moved, keys, (((1,), (1,)), ((), ())), preferred_element_type=jnp.float32
            )
            next_scores[j] = part
            for c in range(0, part.shape[1], LANES):
                piece = part[:, c:c + LANES]
                top = piece if top is None else jnp.maximum(top, piece)
        if now is not None:
            tile, scores, maxima = now
            index = jnp.clip(list_ref[tile, j] - first, 0, last)
            weights = jnp.concatenate(
                [
                    jnp.exp(scores[j, :, c:c + LANES] - maxima[...]).astype(jnp.bfloat16)
                    for c in range(0, scores.shape[2], LANES)
                ],
                axis=1,
            )
            values = window[index, :, value_at:value_at + LANES]
            lane = lax.broadcasted_iota(jnp.int32, values.shape, 1)
            ones = lane >= HEAD_DIM if head == 0 else lane < HEAD_DIM
            values = jnp.where(ones, jnp.ones_like(values), values)
            part = jnp.dot(weights, values, preferred_element_type=jnp.float32)
            total = part if total is None else total + part
    if later is not None:
        next_maxima[...] = jnp.broadcast_to(jnp.max(top, axis=1, keepdims=True), top.shape)
    if now is not None:
        return total / pltpu.roll(total, HEAD_DIM, 1)


def kernel(ulys, blks, units, stages, unit_width, list_hbm, qkv_ref, out_ref, *scratch):
    count = len(stages)
    wins = scratch[:count]
    outs = scratch[count:count + units]
    (scores_a, scores_b, maxima_a, maxima_b, list_ref, list_sem, own_sem, in_send, in_recv, halo_send, halo_recv,
     out_own, out_send, out_recv) = scratch[count + units:]
    list_copy = pltpu.make_async_copy(list_hbm, list_ref, list_sem)
    list_copy.start()
    me = lax.axis_index("uly")
    blk = lax.axis_index("blk")
    first = (blk - 1) * ulys
    has_prev = blk > 0
    has_next = blk < blks - 1

    def peer(step):
        return flip(me, ulys - 1 - step, ulys)

    def mixed(step):
        half, odd = lax.div(step, 2), lax.rem(step, 2)
        return flip(me, odd * (half + 1) + (1 - odd) * (ulys - 1 - half), ulys)

    def near(step):
        return flip(me, step + 1, ulys)

    def columns(owner, stage):
        unit, _, begin, width = stages[stage]
        start = (owner * units + unit) * unit_width + begin
        return qkv_ref.at[:, pl.ds(pl.multiple_of(start, LANES), width)]

    def inbound(stage, other):
        return pltpu.make_async_remote_copy(
            src_ref=columns(other, stage),
            dst_ref=wins[stage].at[ulys + me],
            send_sem=in_send.at[stage, other],
            recv_sem=in_recv.at[stage, me],
            device_id={"uly": other},
            device_id_type=MESH,
        )

    def arrival(stage, other):
        return pltpu.make_async_remote_copy(
            src_ref=columns(other, stage),
            dst_ref=wins[stage].at[ulys + other],
            send_sem=in_send.at[stage, other],
            recv_sem=in_recv.at[stage, other],
            device_id={"uly": other},
            device_id_type=MESH,
        )

    def own(stage):
        return pltpu.make_async_copy(
            columns(me, stage), wins[stage].at[ulys + me], own_sem.at[stage]
        )

    def halo(stage, side, tile):
        return pltpu.make_async_remote_copy(
            src_ref=wins[stage].at[ulys + tile],
            dst_ref=wins[stage].at[2 * ulys * side + tile],
            send_sem=halo_send.at[stage, side, tile],
            recv_sem=halo_recv.at[stage, side, tile],
            device_id={"blk": blk + 1 - 2 * side},
            device_id_type=MESH,
        )

    def out_columns(owner, unit):
        start = (owner * units + unit) * LANES
        return out_ref.at[:, pl.ds(pl.multiple_of(start, LANES), LANES)]

    def outbound(unit, other):
        return pltpu.make_async_remote_copy(
            src_ref=outs[unit].at[other],
            dst_ref=out_columns(me, unit),
            send_sem=out_send.at[unit, other],
            recv_sem=out_recv.at[unit, me],
            device_id={"uly": other},
            device_id_type=MESH,
        )

    def returned(unit, other):
        return pltpu.make_async_remote_copy(
            src_ref=outs[unit].at[other],
            dst_ref=out_columns(other, unit),
            send_sem=out_send.at[unit, other],
            recv_sem=out_recv.at[unit, other],
            device_id={"uly": other},
            device_id_type=MESH,
        )

    def out_here(unit):
        return pltpu.make_async_copy(
            outs[unit].at[me], out_columns(me, unit), out_own.at[unit]
        )

    def forward(stage, tile):
        @pl.when(has_next)
        def _():
            halo(stage, 0, tile).start()

        @pl.when(has_prev)
        def _():
            halo(stage, 1, tile).start()

    def steps(limit, body):
        def run(step, carry):
            body(step)
            return carry
        lax.fori_loop(0, limit, run, 0)

    barrier = pltpu.get_barrier_semaphore()

    def greet(step):
        pl.semaphore_signal(
            barrier, inc=1, device_id={"uly": peer(step)}, device_id_type=MESH
        )

    steps(ulys - 1, greet)

    @pl.when(has_next)
    def _():
        pl.semaphore_signal(barrier, inc=1, device_id={"blk": blk + 1}, device_id_type=MESH)

    @pl.when(has_prev)
    def _():
        pl.semaphore_signal(barrier, inc=1, device_id={"blk": blk - 1}, device_id_type=MESH)

    beside = jnp.where(has_prev, 1, 0) + jnp.where(has_next, 1, 0)
    pl.semaphore_wait(barrier, ulys - 1 + beside)

    for stage in range(min(AHEAD, count)):
        steps(ulys - 1, lambda step, stage=stage: inbound(stage, mixed(step)).start())
    for stage in range(count):
        own(stage).start()

    def closes(stage):
        return stage == count - 1 or stages[stage + 1][0] != stages[stage][0]

    def attend(stage, now, later):
        unit, head, _, _ = stages[stage]
        tile = None
        if now is not None:
            tile = peer(now[0])
            now = (tile,) + now[1:]
        if later is not None:
            following = peer(later[0])
            if head == 0:
                query = wins[stage][ulys + following, :, 0:LANES]
            else:
                query = wins[stage - 1][ulys + following, :, LANES:2 * LANES]
            later = (following, query) + later[1:]
        value_at = LANES if head == 0 else 0
        result = attend_step(
            list_ref, first, wins[stage], value_at, head, now, later
        )
        if tile is None:
            return
        lane = lax.broadcasted_iota(jnp.int32, result.shape, 1)
        if head == 0:
            outs[unit][tile] = jnp.where(lane < HEAD_DIM, result, 0.0).astype(jnp.bfloat16)
        else:
            before = outs[unit][tile].astype(jnp.float32)
            outs[unit][tile] = jnp.where(lane < HEAD_DIM, before, result).astype(jnp.bfloat16)

    def give(stage, step):
        unit = stages[stage][0]
        if closes(stage):
            @pl.when(step < ulys - 1)
            def _():
                outbound(unit, peer(step)).start()

            @pl.when(step == ulys - 1)
            def _():
                out_here(unit).start()

    list_copy.wait()
    for turn in range(count + 1):
        done = turn - 1
        if turn < count:
            own(turn).wait()
            forward(turn, me)
        if done >= 0:
            def arrived(tile, done=done):
                @pl.when(has_prev)
                def _():
                    halo(done, 0, tile).wait_recv()

                @pl.when(has_next)
                def _():
                    halo(done, 1, tile).wait_recv()

            steps(ulys, arrived)

        def take(step, turn=turn):
            source = near(step)
            arrival(turn, source).wait_recv()
            forward(turn, source)

        if done >= 0:
            attend(done, None, (0, scores_a, maxima_a))

        def body(pair, turn=turn, done=done):
            if done >= 0:
                even = 2 * pair
                after = jnp.minimum(even + 2, ulys - 1)
                attend(done, (even, scores_a, maxima_a), (even + 1, scores_b, maxima_b))
                give(done, even)
                attend(done, (even + 1, scores_b, maxima_b), (after, scores_a, maxima_a))
                give(done, even + 1)
            if turn < count:
                @pl.when(pair < ulys // 2 - 1)
                def _():
                    take(pair)

        steps(ulys // 2, body)
        if turn < count:
            steps(ulys // 2, lambda step, take=take: take(step + ulys // 2 - 1))

    def finish(step):
        other = peer(step)
        for stage in range(count):
            inbound(stage, other).wait_send()
        for unit in range(units):
            outbound(unit, other).wait_send()
            returned(unit, other).wait_recv()

    steps(ulys - 1, finish)

    def finish_halo(tile):
        for stage in range(count):
            @pl.when(has_next)
            def _():
                halo(stage, 0, tile).wait_send()

            @pl.when(has_prev)
            def _():
                halo(stage, 1, tile).wait_send()

    steps(ulys, finish_halo)
    for unit in range(units):
        out_here(unit).wait()


def on_device(qkv, tile_list):
    tokens, width = qkv.shape
    ulys, blks = lax.axis_size("uly"), lax.axis_size("blk")
    heads = width // (3 * HEAD_DIM)
    heads_here = heads // ulys
    paired = heads_here % 2 == 0
    if paired:
        units, unit_width = heads_here // 2, 6 * HEAD_DIM
        stages = []
        for unit in range(units):
            stages += [(unit, 0, 0, 2 * LANES), (unit, 1, 2 * LANES, LANES)]
    else:
        units, unit_width = heads_here, 4 * HEAD_DIM
        stages = [(unit, 0, 0, 2 * LANES) for unit in range(units)]
        qkv = jnp.pad(
            qkv.reshape(tokens, heads, 3 * HEAD_DIM), ((0, 0), (0, 0), (0, HEAD_DIM))
        ).reshape(tokens, heads * unit_width)
    listed = tile_list.shape[1]
    count = len(stages)
    out_width = ulys * units * LANES
    dma = pltpu.SemaphoreType.DMA
    pairs = ulys * listed * heads_here
    out = pl.pallas_call(
        functools.partial(kernel, ulys, blks, units, tuple(stages), unit_width),
        out_shape=jax.ShapeDtypeStruct((tokens, out_width), jnp.bfloat16),
        in_specs=[
            pl.BlockSpec(memory_space=pltpu.HBM),
            pl.BlockSpec(memory_space=pltpu.HBM),
        ],
        out_specs=pl.BlockSpec(memory_space=pl.ANY),
        scratch_shapes=[
            pltpu.VMEM((3 * ulys, tokens, stage[3]), jnp.bfloat16) for stage in stages
        ] + [
            pltpu.VMEM((ulys, tokens, LANES), jnp.bfloat16) for _ in range(units)
        ] + [
            pltpu.VMEM((listed, tokens, tokens), jnp.float32),
            pltpu.VMEM((listed, tokens, tokens), jnp.float32),
            pltpu.VMEM((tokens, LANES), jnp.float32),
            pltpu.VMEM((tokens, LANES), jnp.float32),
            pltpu.SMEM(tile_list.shape, jnp.int32),
            dma(()),
            dma((count,)),
            dma((count, ulys)),
            dma((count, ulys)),
            dma((count, 2, ulys)),
            dma((count, 2, ulys)),
            dma((units,)),
            dma((units, ulys)),
            dma((units, ulys)),
        ],
        compiler_params=pltpu.CompilerParams(
            collective_id=0, has_side_effects=True, vmem_limit_bytes=50 * 1024 * 1024
        ),
        cost_estimate=pl.CostEstimate(
            flops=4 * pairs * tokens * tokens * HEAD_DIM,
            bytes_accessed=2 * qkv.size * 2,
            transcendentals=pairs * tokens * tokens,
        ),
    )(tile_list, qkv)
    if not paired:
        out = out.reshape(tokens, heads, LANES)[:, :, :HEAD_DIM]
        out = out.reshape(tokens, heads * HEAD_DIM)
    return out


def solution(mesh):
    in_specs = (P(("blk", "uly"), None), P("blk", None))
    out_specs = P(("blk", "uly"), None)
    return jax.shard_map(
        on_device, mesh=mesh, in_specs=in_specs, out_specs=out_specs, check_vma=False
    )
```

```python
import functools

import jax
import jax.numpy as jnp
from jax import lax
from jax.experimental import pallas as pl
from jax.experimental.pallas import tpu as pltpu
from jax.sharding import PartitionSpec as P

HEAD_DIM = 64
LANES = 128
MESH = pl.DeviceIdType.MESH
SCORE_SCALE = HEAD_DIM ** -0.5
AHEAD = 4


def flip(me, mask, count):
    total, weight = 0, 1
    while weight < count:
        bit = lax.rem(lax.div(me, weight) + lax.div(mask, weight), 2)
        total = total + bit * weight
        weight *= 2
    return total


def attend_tile(list_ref, tile, first, query, wins, stage, head, scores):
    listed = list_ref.shape[1]
    lane = lax.broadcasted_iota(jnp.int32, query.shape, 1)
    moved = pltpu.roll(query.astype(jnp.float32), HEAD_DIM, 1) * SCORE_SCALE
    keep = lane >= HEAD_DIM if head == 0 else lane < HEAD_DIM
    moved = jnp.where(keep, moved, 0.0).astype(jnp.bfloat16)
    values_low = head == 0
    begin = wins[stage].shape[2] - LANES
    top = None
    for j in range(listed):
        index = jnp.clip(list_ref[tile, j] - first, 0, wins[stage].shape[0] - 1)
        keys = wins[stage][index, :, begin:begin + LANES]
        part = lax.dot_general(
            moved, keys, (((1,), (1,)), ((), ())), preferred_element_type=jnp.float32
        )
        scores[j] = part
        for c in range(0, part.shape[1], LANES):
            piece = part[:, c:c + LANES]
            top = piece if top is None else jnp.maximum(top, piece)
    row_max = jnp.max(top, axis=1, keepdims=True)
    total = None
    for j in range(listed):
        index = jnp.clip(list_ref[tile, j] - first, 0, wins[stage].shape[0] - 1)
        weights = jnp.exp(scores[j] - row_max).astype(jnp.bfloat16)
        values = wins[stage][index, :, begin:begin + LANES]
        value_lane = lax.broadcasted_iota(jnp.int32, values.shape, 1)
        ones = value_lane >= HEAD_DIM if values_low else value_lane < HEAD_DIM
        values = jnp.where(ones, jnp.ones_like(values), values)
        part = lax.dot_general(
            weights, values, (((1,), (0,)), ((), ())), preferred_element_type=jnp.float32
        )
        total = part if total is None else total + part
    return total / pltpu.roll(total, HEAD_DIM, 1)


def kernel(ulys, blks, units, stages, unit_width, list_hbm, qkv_hbm, out_ref, *scratch):
    count = len(stages)
    wins = scratch[:count]
    outs = scratch[count:count + units]
    (scores, qkv_ref, qkv_sem, list_ref, list_sem, own_sem, in_send, in_recv, halo_send, halo_recv,
     out_own, out_send, out_recv) = scratch[count + units:]
    list_copy = pltpu.make_async_copy(list_hbm, list_ref, list_sem)
    list_copy.start()
    qkv_copy = pltpu.make_async_copy(qkv_hbm, qkv_ref, qkv_sem)
    qkv_copy.start()
    me = lax.axis_index("uly")
    blk = lax.axis_index("blk")
    first = (blk - 1) * ulys
    has_prev = blk > 0
    has_next = blk < blks - 1

    def peer(step):
        return flip(me, ulys - 1 - step, ulys)

    def mixed(step):
        half, odd = lax.div(step, 2), lax.rem(step, 2)
        return flip(me, odd * (half + 1) + (1 - odd) * (ulys - 1 - half), ulys)

    def near(step):
        return flip(me, step + 1, ulys)

    def columns(owner, stage):
        unit, _, begin, width = stages[stage]
        start = (owner * units + unit) * unit_width + begin
        return qkv_ref.at[:, pl.ds(pl.multiple_of(start, LANES), width)]

    def inbound(stage, other):
        return pltpu.make_async_remote_copy(
            src_ref=columns(other, stage),
            dst_ref=wins[stage].at[ulys + me],
            send_sem=in_send.at[stage, other],
            recv_sem=in_recv.at[stage, me],
            device_id={"uly": other},
            device_id_type=MESH,
        )

    def arrival(stage, other):
        return pltpu.make_async_remote_copy(
            src_ref=columns(other, stage),
            dst_ref=wins[stage].at[ulys + other],
            send_sem=in_send.at[stage, other],
            recv_sem=in_recv.at[stage, other],
            device_id={"uly": other},
            device_id_type=MESH,
        )

    def own(stage):
        return pltpu.make_async_copy(
            columns(me, stage), wins[stage].at[ulys + me], own_sem.at[stage]
        )

    def halo(stage, side, tile):
        width = stages[stage][3]
        pair = pl.ds(width - LANES, LANES)
        return pltpu.make_async_remote_copy(
            src_ref=wins[stage].at[ulys + tile, :, pair],
            dst_ref=wins[stage].at[2 * ulys * side + tile, :, pair],
            send_sem=halo_send.at[stage, side, tile],
            recv_sem=halo_recv.at[stage, side, tile],
            device_id={"blk": blk + 1 - 2 * side},
            device_id_type=MESH,
        )

    def out_columns(owner, unit):
        start = (owner * units + unit) * LANES
        return out_ref.at[:, pl.ds(pl.multiple_of(start, LANES), LANES)]

    def outbound(unit, other):
        return pltpu.make_async_remote_copy(
            src_ref=outs[unit].at[other],
            dst_ref=out_columns(me, unit),
            send_sem=out_send.at[unit, other],
            recv_sem=out_recv.at[unit, me],
            device_id={"uly": other},
            device_id_type=MESH,
        )

    def returned(unit, other):
        return pltpu.make_async_remote_copy(
            src_ref=outs[unit].at[other],
            dst_ref=out_columns(other, unit),
            send_sem=out_send.at[unit, other],
            recv_sem=out_recv.at[unit, other],
            device_id={"uly": other},
            device_id_type=MESH,
        )

    def out_here(unit):
        return pltpu.make_async_copy(
            outs[unit].at[me], out_columns(me, unit), out_own.at[unit]
        )

    def forward(stage, tile):
        @pl.when(has_next)
        def _():
            halo(stage, 0, tile).start()

        @pl.when(has_prev)
        def _():
            halo(stage, 1, tile).start()

    def steps(limit, body):
        def run(step, carry):
            body(step)
            return carry
        lax.fori_loop(0, limit, run, 0)

    barrier = pltpu.get_barrier_semaphore()

    def greet(step):
        pl.semaphore_signal(
            barrier, inc=1, device_id={"uly": peer(step)}, device_id_type=MESH
        )

    steps(ulys - 1, greet)

    @pl.when(has_next)
    def _():
        pl.semaphore_signal(barrier, inc=1, device_id={"blk": blk + 1}, device_id_type=MESH)

    @pl.when(has_prev)
    def _():
        pl.semaphore_signal(barrier, inc=1, device_id={"blk": blk - 1}, device_id_type=MESH)

    beside = jnp.where(has_prev, 1, 0) + jnp.where(has_next, 1, 0)
    pl.semaphore_wait(barrier, ulys - 1 + beside)

    qkv_copy.wait()

    def regroup(unit):
        start = pl.multiple_of(unit * unit_width, LANES)
        low = qkv_ref[:, pl.ds(start, LANES)]
        high = qkv_ref[:, pl.ds(start + LANES, LANES)]
        left = lax.broadcasted_iota(jnp.int32, low.shape, 1) < HEAD_DIM
        qkv_ref[:, pl.ds(start, LANES)] = jnp.where(left, low, high)
        qkv_ref[:, pl.ds(start + LANES, LANES)] = jnp.where(left, high, low)

    steps(ulys * units, regroup)
    for stage in range(min(AHEAD, count)):
        steps(ulys - 1, lambda step, stage=stage: inbound(stage, mixed(step)).start())
    for stage in range(count):
        own(stage).start()

    def compute(stage, tile):
        unit, head, _, _ = stages[stage]
        if head == 0:
            query = wins[stage][ulys + tile, :, 0:LANES]
        else:
            query = wins[stage - 1][ulys + tile, :, 0:LANES]
        result = attend_tile(list_ref, tile, first, query, wins, stage, head, scores)
        lane = lax.broadcasted_iota(jnp.int32, result.shape, 1)
        if head == 0:
            outs[unit][tile] = jnp.where(lane < HEAD_DIM, result, 0.0).astype(jnp.bfloat16)
        else:
            before = outs[unit][tile].astype(jnp.float32)
            outs[unit][tile] = jnp.where(lane < HEAD_DIM, before, result).astype(jnp.bfloat16)

    list_copy.wait()
    for turn in range(count + 1):
        done = turn - 1
        if turn < count:
            own(turn).wait()
            forward(turn, me)
        if done >= 0:
            def arrived(tile, done=done):
                @pl.when(has_prev)
                def _():
                    halo(done, 0, tile).wait_recv()

                @pl.when(has_next)
                def _():
                    halo(done, 1, tile).wait_recv()

            steps(ulys, arrived)

        def body(step, turn=turn, done=done):
            other = peer(step)
            if turn < count:
                @pl.when(step < ulys - 1)
                def _():
                    source = near(step)
                    arrival(turn, source).wait_recv()
                    forward(turn, source)
                    if turn + AHEAD < count:
                        inbound(turn + AHEAD, source).start()
            if done >= 0:
                compute(done, other)
                unit = stages[done][0]
                if done == count - 1 or stages[done + 1][0] != unit:
                    @pl.when(step < ulys - 1)
                    def _():
                        outbound(unit, other).start()

                    @pl.when(step == ulys - 1)
                    def _():
                        out_here(unit).start()

        steps(ulys, body)

    def finish(step):
        other = peer(step)
        for stage in range(count):
            inbound(stage, other).wait_send()
        for unit in range(units):
            outbound(unit, other).wait_send()
            returned(unit, other).wait_recv()

    steps(ulys - 1, finish)

    def finish_halo(tile):
        for stage in range(count):
            @pl.when(has_next)
            def _():
                halo(stage, 0, tile).wait_send()

            @pl.when(has_prev)
            def _():
                halo(stage, 1, tile).wait_send()

    steps(ulys, finish_halo)
    for unit in range(units):
        out_here(unit).wait()


def on_device(qkv, tile_list):
    tokens, width = qkv.shape
    ulys, blks = lax.axis_size("uly"), lax.axis_size("blk")
    heads = width // (3 * HEAD_DIM)
    heads_here = heads // ulys
    paired = heads_here % 2 == 0
    if paired:
        units, unit_width = heads_here // 2, 6 * HEAD_DIM
        stages = []
        for unit in range(units):
            stages += [(unit, 0, 0, 2 * LANES), (unit, 1, 2 * LANES, LANES)]
    else:
        units, unit_width = heads_here, 4 * HEAD_DIM
        stages = [(unit, 0, 0, 2 * LANES) for unit in range(units)]
        qkv = jnp.pad(
            qkv.reshape(tokens, heads, 3 * HEAD_DIM), ((0, 0), (0, 0), (0, HEAD_DIM))
        ).reshape(tokens, heads * unit_width)
    listed = tile_list.shape[1]
    count = len(stages)
    out_width = ulys * units * LANES
    dma = pltpu.SemaphoreType.DMA
    pairs = ulys * listed * heads_here
    out = pl.pallas_call(
        functools.partial(kernel, ulys, blks, units, tuple(stages), unit_width),
        out_shape=jax.ShapeDtypeStruct((tokens, out_width), jnp.bfloat16),
        in_specs=[
            pl.BlockSpec(memory_space=pltpu.HBM),
            pl.BlockSpec(memory_space=pltpu.HBM),
        ],
        out_specs=pl.BlockSpec(memory_space=pl.ANY),
        scratch_shapes=[
            pltpu.VMEM((3 * ulys, tokens, stage[3]), jnp.bfloat16) for stage in stages
        ] + [
            pltpu.VMEM((ulys, tokens, LANES), jnp.bfloat16) for _ in range(units)
        ] + [
            pltpu.VMEM((listed, tokens, tokens), jnp.float32),
            pltpu.VMEM(qkv.shape, jnp.bfloat16),
            dma(()),
            pltpu.SMEM(tile_list.shape, jnp.int32),
            dma(()),
            dma((count,)),
            dma((count, ulys)),
            dma((count, ulys)),
            dma((count, 2, ulys)),
            dma((count, 2, ulys)),
            dma((units,)),
            dma((units, ulys)),
            dma((units, ulys)),
        ],
        compiler_params=pltpu.CompilerParams(
            collective_id=0, has_side_effects=True, vmem_limit_bytes=50 * 1024 * 1024
        ),
        cost_estimate=pl.CostEstimate(
            flops=4 * pairs * tokens * tokens * HEAD_DIM,
            bytes_accessed=2 * qkv.size * 2,
            transcendentals=pairs * tokens * tokens,
        ),
    )(tile_list, qkv)
    if not paired:
        out = out.reshape(tokens, heads, LANES)[:, :, :HEAD_DIM]
        out = out.reshape(tokens, heads * HEAD_DIM)
    return out


def solution(mesh):
    in_specs = (P(("blk", "uly"), None), P("blk", None))
    out_specs = P(("blk", "uly"), None)
    return jax.shard_map(
        on_device, mesh=mesh, in_specs=in_specs, out_specs=out_specs, check_vma=False
    )
```

```python
import functools

import jax
import jax.numpy as jnp
from jax import lax
from jax.experimental import pallas as pl
from jax.experimental.pallas import tpu as pltpu
from jax.sharding import PartitionSpec as P

HEAD_DIM = 64
LANES = 128
MESH = pl.DeviceIdType.MESH
SCORE_SCALE = HEAD_DIM ** -0.5


def flip(me, mask, count):
    total, weight = 0, 1
    while weight < count:
        bit = lax.rem(lax.div(me, weight) + lax.div(mask, weight), 2)
        total = total + bit * weight
        weight *= 2
    return total


def attend_tile(list_ref, tile, first, query, wins, stage, head, scores):
    listed = list_ref.shape[1]
    lane = lax.broadcasted_iota(jnp.int32, query.shape, 1)
    moved = pltpu.roll(query.astype(jnp.float32), HEAD_DIM, 1) * SCORE_SCALE
    keep = lane >= HEAD_DIM if head == 0 else lane < HEAD_DIM
    moved = jnp.where(keep, moved, 0.0).astype(jnp.bfloat16)
    values_low = head == 0
    begin = wins[stage].shape[2] - LANES
    top = None
    for j in range(listed):
        index = jnp.clip(list_ref[tile, j] - first, 0, wins[stage].shape[0] - 1)
        keys = wins[stage][index, :, begin:begin + LANES]
        part = lax.dot_general(
            moved, keys, (((1,), (1,)), ((), ())), preferred_element_type=jnp.float32
        )
        scores[j] = part
        for c in range(0, part.shape[1], LANES):
            piece = part[:, c:c + LANES]
            top = piece if top is None else jnp.maximum(top, piece)
    row_max = jnp.max(top, axis=1, keepdims=True)
    total = None
    for j in range(listed):
        index = jnp.clip(list_ref[tile, j] - first, 0, wins[stage].shape[0] - 1)
        weights = jnp.exp(scores[j] - row_max).astype(jnp.bfloat16)
        values = wins[stage][index, :, begin:begin + LANES]
        value_lane = lax.broadcasted_iota(jnp.int32, values.shape, 1)
        ones = value_lane >= HEAD_DIM if values_low else value_lane < HEAD_DIM
        values = jnp.where(ones, jnp.ones_like(values), values)
        part = lax.dot_general(
            weights, values, (((1,), (0,)), ((), ())), preferred_element_type=jnp.float32
        )
        total = part if total is None else total + part
    return total / pltpu.roll(total, HEAD_DIM, 1)


def kernel(ulys, blks, units, stages, unit_width, list_hbm, qkv_hbm, out_ref, *scratch):
    count = len(stages)
    wins = scratch[:count]
    outs = scratch[count:count + units]
    relays = scratch[count + units:2 * count + units]
    (relay_send, relay_recv, scores, qkv_ref, qkv_sem, list_ref, list_sem, own_sem, in_send, in_recv, halo_send, halo_recv,
     out_own, out_send, out_recv) = scratch[2 * count + units:]
    list_copy = pltpu.make_async_copy(list_hbm, list_ref, list_sem)
    list_copy.start()
    qkv_copy = pltpu.make_async_copy(qkv_hbm, qkv_ref, qkv_sem)
    qkv_copy.start()
    me = lax.axis_index("uly")
    blk = lax.axis_index("blk")
    first = (blk - 1) * ulys
    has_prev = blk > 0
    has_next = blk < blks - 1

    def peer(step):
        return flip(me, ulys - 1 - step, ulys)

    def near(step):
        return flip(me, step + 1, ulys)

    def columns(owner, stage):
        unit, _, begin, width = stages[stage]
        start = (owner * units + unit) * unit_width + begin
        return qkv_ref.at[:, pl.ds(pl.multiple_of(start, LANES), width)]

    def inbound(stage, other):
        return pltpu.make_async_remote_copy(
            src_ref=columns(other, stage),
            dst_ref=wins[stage].at[ulys + me],
            send_sem=in_send.at[stage, other],
            recv_sem=in_recv.at[stage, me],
            device_id={"uly": other},
            device_id_type=MESH,
        )

    half = ulys // 2
    low = lax.rem(me, 2)
    mine = lax.div(me, 2)
    partner = me + 1 - 2 * low

    def place(step):
        return flip(mine, half - 1 - step, half)

    def first_leg(stage, to):
        owner = 2 * to + 1 - low
        return pltpu.make_async_remote_copy(
            src_ref=columns(owner, stage),
            dst_ref=relays[stage].at[to],
            send_sem=in_send.at[stage, owner],
            recv_sem=relay_recv.at[stage, to],
            device_id={"uly": partner},
            device_id_type=MESH,
        )

    def second_leg(stage, to):
        return pltpu.make_async_remote_copy(
            src_ref=relays[stage].at[to],
            dst_ref=wins[stage].at[ulys + partner],
            send_sem=relay_send.at[stage, to],
            recv_sem=in_recv.at[stage, partner],
            device_id={"uly": 2 * to + low},
            device_id_type=MESH,
        )

    def send_out(stage):
        def one(step):
            first_leg(stage, place(step)).start()
            inbound(stage, 2 * place(step) + low).start()
        steps(half - 1, one)
        inbound(stage, partner).start()

    def pass_on(stage):
        def one(step):
            first_leg(stage, place(step)).wait_recv()
            second_leg(stage, place(step)).start()
        steps(half - 1, one)

    def arrival(stage, other):
        return pltpu.make_async_remote_copy(
            src_ref=columns(other, stage),
            dst_ref=wins[stage].at[ulys + other],
            send_sem=in_send.at[stage, other],
            recv_sem=in_recv.at[stage, other],
            device_id={"uly": other},
            device_id_type=MESH,
        )

    def own(stage):
        return pltpu.make_async_copy(
            columns(me, stage), wins[stage].at[ulys + me], own_sem.at[stage]
        )

    def halo(stage, side, tile):
        width = stages[stage][3]
        pair = pl.ds(width - LANES, LANES)
        return pltpu.make_async_remote_copy(
            src_ref=wins[stage].at[ulys + tile, :, pair],
            dst_ref=wins[stage].at[2 * ulys * side + tile, :, pair],
            send_sem=halo_send.at[stage, side, tile],
            recv_sem=halo_recv.at[stage, side, tile],
            device_id={"blk": blk + 1 - 2 * side},
            device_id_type=MESH,
        )

    def out_columns(owner, unit):
        start = (owner * units + unit) * LANES
        return out_ref.at[:, pl.ds(pl.multiple_of(start, LANES), LANES)]

    def outbound(unit, other):
        return pltpu.make_async_remote_copy(
            src_ref=outs[unit].at[other],
            dst_ref=out_columns(me, unit),
            send_sem=out_send.at[unit, other],
            recv_sem=out_recv.at[unit, me],
            device_id={"uly": other},
            device_id_type=MESH,
        )

    def returned(unit, other):
        return pltpu.make_async_remote_copy(
            src_ref=outs[unit].at[other],
            dst_ref=out_columns(other, unit),
            send_sem=out_send.at[unit, other],
            recv_sem=out_recv.at[unit, other],
            device_id={"uly": other},
            device_id_type=MESH,
        )

    def out_here(unit):
        return pltpu.make_async_copy(
            outs[unit].at[me], out_columns(me, unit), out_own.at[unit]
        )

    def forward(stage, tile):
        @pl.when(has_next)
        def _():
            halo(stage, 0, tile).start()

        @pl.when(has_prev)
        def _():
            halo(stage, 1, tile).start()

    def steps(limit, body):
        def run(step, carry):
            body(step)
            return carry
        lax.fori_loop(0, limit, run, 0)

    barrier = pltpu.get_barrier_semaphore()

    def greet(step):
        pl.semaphore_signal(
            barrier, inc=1, device_id={"uly": peer(step)}, device_id_type=MESH
        )

    steps(ulys - 1, greet)

    @pl.when(has_next)
    def _():
        pl.semaphore_signal(barrier, inc=1, device_id={"blk": blk + 1}, device_id_type=MESH)

    @pl.when(has_prev)
    def _():
        pl.semaphore_signal(barrier, inc=1, device_id={"blk": blk - 1}, device_id_type=MESH)

    beside = jnp.where(has_prev, 1, 0) + jnp.where(has_next, 1, 0)
    pl.semaphore_wait(barrier, ulys - 1 + beside)

    qkv_copy.wait()

    def regroup(unit):
        start = pl.multiple_of(unit * unit_width, LANES)
        low = qkv_ref[:, pl.ds(start, LANES)]
        high = qkv_ref[:, pl.ds(start + LANES, LANES)]
        left = lax.broadcasted_iota(jnp.int32, low.shape, 1) < HEAD_DIM
        qkv_ref[:, pl.ds(start, LANES)] = jnp.where(left, low, high)
        qkv_ref[:, pl.ds(start + LANES, LANES)] = jnp.where(left, high, low)

    steps(ulys * units, regroup)
    for stage in range(count):
        send_out(stage)
    for stage in range(count):
        own(stage).start()

    def compute(stage, tile):
        unit, head, _, _ = stages[stage]
        if head == 0:
            query = wins[stage][ulys + tile, :, 0:LANES]
        else:
            query = wins[stage - 1][ulys + tile, :, 0:LANES]
        result = attend_tile(list_ref, tile, first, query, wins, stage, head, scores)
        lane = lax.broadcasted_iota(jnp.int32, result.shape, 1)
        if head == 0:
            outs[unit][tile] = jnp.where(lane < HEAD_DIM, result, 0.0).astype(jnp.bfloat16)
        else:
            before = outs[unit][tile].astype(jnp.float32)
            outs[unit][tile] = jnp.where(lane < HEAD_DIM, before, result).astype(jnp.bfloat16)

    list_copy.wait()
    for stage in range(min(2, count)):
        pass_on(stage)
    for turn in range(count + 1):
        done = turn - 1
        if turn < count:
            if turn + 2 < count:
                pass_on(turn + 2)
            own(turn).wait()
            forward(turn, me)
        if done >= 0:
            def arrived(tile, done=done):
                @pl.when(has_prev)
                def _():
                    halo(done, 0, tile).wait_recv()

                @pl.when(has_next)
                def _():
                    halo(done, 1, tile).wait_recv()

            steps(ulys, arrived)

        def body(step, turn=turn, done=done):
            other = peer(step)
            if turn < count:
                @pl.when(step < ulys - 1)
                def _():
                    source = near(step)
                    arrival(turn, source).wait_recv()
                    forward(turn, source)
            if done >= 0:
                compute(done, other)
                unit = stages[done][0]
                if done == count - 1 or stages[done + 1][0] != unit:
                    @pl.when(step < ulys - 1)
                    def _():
                        outbound(unit, other).start()

                    @pl.when(step == ulys - 1)
                    def _():
                        out_here(unit).start()

        steps(ulys, body)

    def finish(step):
        other = peer(step)
        for stage in range(count):
            inbound(stage, other).wait_send()
        for unit in range(units):
            outbound(unit, other).wait_send()
            returned(unit, other).wait_recv()

    steps(ulys - 1, finish)

    def finish_halo(tile):
        for stage in range(count):
            @pl.when(has_next)
            def _():
                halo(stage, 0, tile).wait_send()

            @pl.when(has_prev)
            def _():
                halo(stage, 1, tile).wait_send()

    steps(ulys, finish_halo)

    def finish_legs(step):
        for stage in range(count):
            second_leg(stage, place(step)).wait_send()

    steps(half - 1, finish_legs)
    for unit in range(units):
        out_here(unit).wait()


def on_device(qkv, tile_list):
    tokens, width = qkv.shape
    ulys, blks = lax.axis_size("uly"), lax.axis_size("blk")
    heads = width // (3 * HEAD_DIM)
    heads_here = heads // ulys
    paired = heads_here % 2 == 0
    if paired:
        units, unit_width = heads_here // 2, 6 * HEAD_DIM
        stages = []
        for unit in range(units):
            stages += [(unit, 0, 0, 2 * LANES), (unit, 1, 2 * LANES, LANES)]
    else:
        units, unit_width = heads_here, 4 * HEAD_DIM
        stages = [(unit, 0, 0, 2 * LANES) for unit in range(units)]
        qkv = jnp.pad(
            qkv.reshape(tokens, heads, 3 * HEAD_DIM), ((0, 0), (0, 0), (0, HEAD_DIM))
        ).reshape(tokens, heads * unit_width)
    listed = tile_list.shape[1]
    count = len(stages)
    out_width = ulys * units * LANES
    dma = pltpu.SemaphoreType.DMA
    pairs = ulys * listed * heads_here
    out = pl.pallas_call(
        functools.partial(kernel, ulys, blks, units, tuple(stages), unit_width),
        out_shape=jax.ShapeDtypeStruct((tokens, out_width), jnp.bfloat16),
        in_specs=[
            pl.BlockSpec(memory_space=pltpu.HBM),
            pl.BlockSpec(memory_space=pltpu.HBM),
        ],
        out_specs=pl.BlockSpec(memory_space=pl.ANY),
        scratch_shapes=[
            pltpu.VMEM((3 * ulys, tokens, stage[3]), jnp.bfloat16) for stage in stages
        ] + [
            pltpu.VMEM((ulys, tokens, LANES), jnp.bfloat16) for _ in range(units)
        ] + [
            pltpu.VMEM((ulys // 2, tokens, stage[3]), jnp.bfloat16) for stage in stages
        ] + [
            dma((count, ulys // 2)),
            dma((count, ulys // 2)),
            pltpu.VMEM((listed, tokens, tokens), jnp.float32),
            pltpu.VMEM(qkv.shape, jnp.bfloat16),
            dma(()),
            pltpu.SMEM(tile_list.shape, jnp.int32),
            dma(()),
            dma((count,)),
            dma((count, ulys)),
            dma((count, ulys)),
            dma((count, 2, ulys)),
            dma((count, 2, ulys)),
            dma((units,)),
            dma((units, ulys)),
            dma((units, ulys)),
        ],
        compiler_params=pltpu.CompilerParams(
            collective_id=0, has_side_effects=True, vmem_limit_bytes=50 * 1024 * 1024
        ),
        cost_estimate=pl.CostEstimate(
            flops=4 * pairs * tokens * tokens * HEAD_DIM,
            bytes_accessed=2 * qkv.size * 2,
            transcendentals=pairs * tokens * tokens,
        ),
    )(tile_list, qkv)
    if not paired:
        out = out.reshape(tokens, heads, LANES)[:, :, :HEAD_DIM]
        out = out.reshape(tokens, heads * HEAD_DIM)
    return out


def solution(mesh):
    in_specs = (P(("blk", "uly"), None), P("blk", None))
    out_specs = P(("blk", "uly"), None)
    return jax.shard_map(
        on_device, mesh=mesh, in_specs=in_specs, out_specs=out_specs, check_vma=False
    )
```

```python
import functools

import jax
import jax.numpy as jnp
from jax import lax
from jax.experimental import pallas as pl
from jax.experimental.pallas import tpu as pltpu
from jax.sharding import PartitionSpec as P

HEAD_DIM = 64
LANES = 128
MESH = pl.DeviceIdType.MESH
SCORE_SCALE = HEAD_DIM ** -0.5
AHEAD = 4


def flip(me, mask, count):
    total, weight = 0, 1
    while weight < count:
        bit = lax.rem(lax.div(me, weight) + lax.div(mask, weight), 2)
        total = total + bit * weight
        weight *= 2
    return total


def attend_tile(list_ref, tile, first, query, wins, stage, head, scores):
    listed = list_ref.shape[1]
    lane = lax.broadcasted_iota(jnp.int32, query.shape, 1)
    moved = pltpu.roll(query.astype(jnp.float32), HEAD_DIM, 1) * SCORE_SCALE
    keep = lane >= HEAD_DIM if head == 0 else lane < HEAD_DIM
    moved = jnp.where(keep, moved, 0.0).astype(jnp.bfloat16)
    values_low = head == 0
    begin = wins[stage].shape[2] - LANES
    top = None
    for j in range(listed):
        index = jnp.clip(list_ref[tile, j] - first, 0, wins[stage].shape[0] - 1)
        keys = wins[stage][index, :, begin:begin + LANES]
        part = lax.dot_general(
            moved, keys, (((1,), (1,)), ((), ())), preferred_element_type=jnp.float32
        )
        scores[j] = part
        for c in range(0, part.shape[1], LANES):
            piece = part[:, c:c + LANES]
            top = piece if top is None else jnp.maximum(top, piece)
    row_max = jnp.max(top, axis=1, keepdims=True)
    total = None
    for j in range(listed):
        index = jnp.clip(list_ref[tile, j] - first, 0, wins[stage].shape[0] - 1)
        weights = jnp.exp(scores[j] - row_max).astype(jnp.bfloat16)
        values = wins[stage][index, :, begin:begin + LANES]
        value_lane = lax.broadcasted_iota(jnp.int32, values.shape, 1)
        ones = value_lane >= HEAD_DIM if values_low else value_lane < HEAD_DIM
        values = jnp.where(ones, jnp.ones_like(values), values)
        part = lax.dot_general(
            weights, values, (((1,), (0,)), ((), ())), preferred_element_type=jnp.float32
        )
        total = part if total is None else total + part
    return total / pltpu.roll(total, HEAD_DIM, 1)


def kernel(ulys, blks, units, stages, unit_width, list_hbm, qkv_hbm, out_ref, *scratch):
    count = len(stages)
    wins = scratch[:count]
    outs = scratch[count:count + units]
    (scores, qkv_ref, qkv_sem, list_ref, list_sem, own_sem, in_send, in_recv, halo_send, halo_recv,
     out_own, out_send, out_recv) = scratch[count + units:]
    list_copy = pltpu.make_async_copy(list_hbm, list_ref, list_sem)
    list_copy.start()
    qkv_copy = pltpu.make_async_copy(qkv_hbm, qkv_ref, qkv_sem)
    qkv_copy.start()
    me = lax.axis_index("uly")
    blk = lax.axis_index("blk")
    first = (blk - 1) * ulys
    has_prev = blk > 0
    has_next = blk < blks - 1

    def peer(step):
        return flip(me, ulys - 1 - step, ulys)

    def mixed(step):
        half, odd = lax.div(step, 2), lax.rem(step, 2)
        return flip(me, odd * (half + 1) + (1 - odd) * (ulys - 1 - half), ulys)

    def near(step):
        return flip(me, step + 1, ulys)

    def columns(owner, stage):
        unit, _, begin, width = stages[stage]
        start = (owner * units + unit) * unit_width + begin
        return qkv_ref.at[:, pl.ds(pl.multiple_of(start, LANES), width)]

    def inbound(stage, other):
        return pltpu.make_async_remote_copy(
            src_ref=columns(other, stage),
            dst_ref=wins[stage].at[ulys + me],
            send_sem=in_send.at[stage, other],
            recv_sem=in_recv.at[stage, me],
            device_id={"uly": other},
            device_id_type=MESH,
        )

    def arrival(stage, other):
        return pltpu.make_async_remote_copy(
            src_ref=columns(other, stage),
            dst_ref=wins[stage].at[ulys + other],
            send_sem=in_send.at[stage, other],
            recv_sem=in_recv.at[stage, other],
            device_id={"uly": other},
            device_id_type=MESH,
        )

    def own(stage):
        return pltpu.make_async_copy(
            columns(me, stage), wins[stage].at[ulys + me], own_sem.at[stage]
        )

    def halo(stage, side, tile):
        width = stages[stage][3]
        pair = pl.ds(width - LANES, LANES)
        return pltpu.make_async_remote_copy(
            src_ref=wins[stage].at[ulys + tile, :, pair],
            dst_ref=wins[stage].at[2 * ulys * side + tile, :, pair],
            send_sem=halo_send.at[stage, side, tile],
            recv_sem=halo_recv.at[stage, side, tile],
            device_id={"blk": blk + 1 - 2 * side},
            device_id_type=MESH,
        )

    def out_columns(owner, unit):
        start = (owner * units + unit) * LANES
        return out_ref.at[:, pl.ds(pl.multiple_of(start, LANES), LANES)]

    def outbound(unit, other):
        return pltpu.make_async_remote_copy(
            src_ref=outs[unit].at[other],
            dst_ref=out_columns(me, unit),
            send_sem=out_send.at[unit, other],
            recv_sem=out_recv.at[unit, me],
            device_id={"uly": other},
            device_id_type=MESH,
        )

    def returned(unit, other):
        return pltpu.make_async_remote_copy(
            src_ref=outs[unit].at[other],
            dst_ref=out_columns(other, unit),
            send_sem=out_send.at[unit, other],
            recv_sem=out_recv.at[unit, other],
            device_id={"uly": other},
            device_id_type=MESH,
        )

    def out_here(unit):
        return pltpu.make_async_copy(
            outs[unit].at[me], out_columns(me, unit), out_own.at[unit]
        )

    def forward(stage, tile):
        @pl.when(has_next)
        def _():
            halo(stage, 0, tile).start()

        @pl.when(has_prev)
        def _():
            halo(stage, 1, tile).start()

    def steps(limit, body):
        def run(step, carry):
            body(step)
            return carry
        lax.fori_loop(0, limit, run, 0)

    barrier = pltpu.get_barrier_semaphore()

    def greet(step):
        pl.semaphore_signal(
            barrier, inc=1, device_id={"uly": peer(step)}, device_id_type=MESH
        )

    steps(ulys - 1, greet)

    @pl.when(has_next)
    def _():
        pl.semaphore_signal(barrier, inc=1, device_id={"blk": blk + 1}, device_id_type=MESH)

    @pl.when(has_prev)
    def _():
        pl.semaphore_signal(barrier, inc=1, device_id={"blk": blk - 1}, device_id_type=MESH)

    beside = jnp.where(has_prev, 1, 0) + jnp.where(has_next, 1, 0)
    pl.semaphore_wait(barrier, ulys - 1 + beside)

    qkv_copy.wait()

    def regroup(unit):
        start = pl.multiple_of(unit * unit_width, LANES)
        low = qkv_ref[:, pl.ds(start, LANES)]
        high = qkv_ref[:, pl.ds(start + LANES, LANES)]
        left = lax.broadcasted_iota(jnp.int32, low.shape, 1) < HEAD_DIM
        qkv_ref[:, pl.ds(start, LANES)] = jnp.where(left, low, high)
        qkv_ref[:, pl.ds(start + LANES, LANES)] = jnp.where(left, high, low)

    steps(ulys * units, regroup)
    for stage in range(min(AHEAD, count)):
        steps(ulys - 1, lambda step, stage=stage: inbound(stage, mixed(step)).start())
    for stage in range(count):
        own(stage).start()

    def compute(stage, tile):
        unit, head, _, _ = stages[stage]
        if head == 0:
            query = wins[stage][ulys + tile, :, 0:LANES]
        else:
            query = wins[stage - 1][ulys + tile, :, 0:LANES]
        result = attend_tile(list_ref, tile, first, query, wins, stage, head, scores)
        lane = lax.broadcasted_iota(jnp.int32, result.shape, 1)
        if head == 0:
            outs[unit][tile] = jnp.where(lane < HEAD_DIM, result, 0.0).astype(jnp.bfloat16)
        else:
            before = outs[unit][tile].astype(jnp.float32)
            outs[unit][tile] = jnp.where(lane < HEAD_DIM, before, result).astype(jnp.bfloat16)

    list_copy.wait()
    for turn in range(count + 1):
        done = turn - 1
        if turn < count:
            own(turn).wait()
            forward(turn, me)
        if done >= 0:
            def arrived(tile, done=done):
                @pl.when(has_prev)
                def _():
                    halo(done, 0, tile).wait_recv()

                @pl.when(has_next)
                def _():
                    halo(done, 1, tile).wait_recv()

            steps(ulys, arrived)

        def take(step, turn=turn):
            source = near(step)
            arrival(turn, source).wait_recv()
            forward(turn, source)

        def body(step, turn=turn, done=done):
            other = peer(step)
            if done >= 0:
                compute(done, other)
                unit = stages[done][0]
                if done == count - 1 or stages[done + 1][0] != unit:
                    @pl.when(step < ulys - 1)
                    def _():
                        outbound(unit, other).start()

                    @pl.when(step == ulys - 1)
                    def _():
                        out_here(unit).start()

            if turn < count:
                @pl.when(step < ulys // 2 - 1)
                def _():
                    take(step)

        steps(ulys, body)
        if turn < count:
            steps(ulys // 2, lambda step, take=take: take(step + ulys // 2 - 1))

    def finish(step):
        other = peer(step)
        for stage in range(count):
            inbound(stage, other).wait_send()
        for unit in range(units):
            outbound(unit, other).wait_send()
            returned(unit, other).wait_recv()

    steps(ulys - 1, finish)

    def finish_halo(tile):
        for stage in range(count):
            @pl.when(has_next)
            def _():
                halo(stage, 0, tile).wait_send()

            @pl.when(has_prev)
            def _():
                halo(stage, 1, tile).wait_send()

    steps(ulys, finish_halo)
    for unit in range(units):
        out_here(unit).wait()


def on_device(qkv, tile_list):
    tokens, width = qkv.shape
    ulys, blks = lax.axis_size("uly"), lax.axis_size("blk")
    heads = width // (3 * HEAD_DIM)
    heads_here = heads // ulys
    paired = heads_here % 2 == 0
    if paired:
        units, unit_width = heads_here // 2, 6 * HEAD_DIM
        stages = []
        for unit in range(units):
            stages += [(unit, 0, 0, 2 * LANES), (unit, 1, 2 * LANES, LANES)]
    else:
        units, unit_width = heads_here, 4 * HEAD_DIM
        stages = [(unit, 0, 0, 2 * LANES) for unit in range(units)]
        qkv = jnp.pad(
            qkv.reshape(tokens, heads, 3 * HEAD_DIM), ((0, 0), (0, 0), (0, HEAD_DIM))
        ).reshape(tokens, heads * unit_width)
    listed = tile_list.shape[1]
    count = len(stages)
    out_width = ulys * units * LANES
    dma = pltpu.SemaphoreType.DMA
    pairs = ulys * listed * heads_here
    out = pl.pallas_call(
        functools.partial(kernel, ulys, blks, units, tuple(stages), unit_width),
        out_shape=jax.ShapeDtypeStruct((tokens, out_width), jnp.bfloat16),
        in_specs=[
            pl.BlockSpec(memory_space=pltpu.HBM),
            pl.BlockSpec(memory_space=pltpu.HBM),
        ],
        out_specs=pl.BlockSpec(memory_space=pl.ANY),
        scratch_shapes=[
            pltpu.VMEM((3 * ulys, tokens, stage[3]), jnp.bfloat16) for stage in stages
        ] + [
            pltpu.VMEM((ulys, tokens, LANES), jnp.bfloat16) for _ in range(units)
        ] + [
            pltpu.VMEM((listed, tokens, tokens), jnp.float32),
            pltpu.VMEM(qkv.shape, jnp.bfloat16),
            dma(()),
            pltpu.SMEM(tile_list.shape, jnp.int32),
            dma(()),
            dma((count,)),
            dma((count, ulys)),
            dma((count, ulys)),
            dma((count, 2, ulys)),
            dma((count, 2, ulys)),
            dma((units,)),
            dma((units, ulys)),
            dma((units, ulys)),
        ],
        compiler_params=pltpu.CompilerParams(
            collective_id=0, has_side_effects=True, vmem_limit_bytes=50 * 1024 * 1024
        ),
        cost_estimate=pl.CostEstimate(
            flops=4 * pairs * tokens * tokens * HEAD_DIM,
            bytes_accessed=2 * qkv.size * 2,
            transcendentals=pairs * tokens * tokens,
        ),
    )(tile_list, qkv)
    if not paired:
        out = out.reshape(tokens, heads, LANES)[:, :, :HEAD_DIM]
        out = out.reshape(tokens, heads * HEAD_DIM)
    return out


def solution(mesh):
    in_specs = (P(("blk", "uly"), None), P("blk", None))
    out_specs = P(("blk", "uly"), None)
    return jax.shard_map(
        on_device, mesh=mesh, in_specs=in_specs, out_specs=out_specs, check_vma=False
    )
```
